32 devices in a mesh: groups: 2 (over y), mem: 4 (over z), comp: 4 (over x, core).
Axes of the slice: x: 2, y: 2, z: 4, core: 2. Of those that a mesh axis runs over, the one named last changes fastest.
Arguments:
- hidden_in: bfloat16 [64, 8192], P('groups', 'mem'), parts along dimension 0, may hold values from -4 to 4
- lengths: int32 [64], P('groups'), parts along dimension 0, may hold values from 1 to 25344, as said below
- block_table: int32 [64, 128], P('groups'), parts along dimension 0, may hold values from 0 to 159, as said below
- cache_keys: bfloat16 [320, 256, 1024], P(('groups', 'mem'), None, 'comp'), parts along dimension 0, may hold values from -300 to 300
- cache_values: bfloat16 [320, 256, 1024], P(('groups', 'mem'), None, 'comp'), parts along dimension 0, may hold values from -6 to 6
- attn_gain: bfloat16 [8192], P('mem'), may hold values from 0.099609375 to 1.8984375
- w_query: bfloat16 [8192, 8192], P('mem', 'comp'), may hold values from -0.0625 to 0.0625
- w_kv: bfloat16 [8192, 2, 1024], P('mem', None, 'comp'), may hold values from -0.0625 to 0.0625
- w_out: bfloat16 [8192, 8192], P('comp', 'mem'), may hold values from -0.0625 to 0.0625
- ffn_gain: bfloat16 [8192], P('mem'), may hold values from 0.099609375 to 1.8984375
- w_gate_up: bfloat16 [8192, 2, 14336], P('mem', None, 'comp'), may hold values from -0.0625 to 0.0625
- w_down: bfloat16 [14336, 8192], P('comp', 'mem'), may hold values from -0.046875 to 0.046875
Outputs:
- attended: bfloat16 [64, 8192], P('groups', 'comp'), parts along dimension 0
- updated: bfloat16 [64, 8192], P('groups', 'mem'), parts along dimension 0
The draws below stay inside these ranges and needn't reach their ends.
There are 2 independent parts, one for each index of `groups`. The reference program is written for one: setup_inputs(seed, part) draws one part's arguments, and reference() takes and returns one part's arrays. A program takes and returns all parts, laid end to end along the dimension named above; an argument that names none is the same for every part. Nothing has to cross between parts.
Inputs may be any that keep to these rules, and one draw needn't show every extreme that they name: `lengths`: one request has the largest length, the others are ragged and shorter. For each block b of request r that holds a position below lengths[r], block_table[r, b] is its slot; slot s belongs to memory device s // 40. Other entries are 0 or 159 and unused. No two used entries share a slot, the used slots of one memory device are its lowest ones, and in every draw some memory device has all 40 of its slots used. Slots that no entry uses hold arbitrary finite values.
All inputs are finite; a program needn't handle non-finite values.
Results may differ from the reference program's by a relative error of at most 0.01.
The reference program's roundings to bfloat16 on the way count: a program that leaves them out, or rounds other values in their place, can miss the bound.
Values may be sent and summed in bfloat16 or wider, within the bound.
No kernel may reach another device: no remote copies, remote signals or barrier semaphores. Data moves between devices by JAX's collectives and lax.ppermute only.
A program may use at most 192 MiB of HBM per device.

```python
import math
import jax
import jax.numpy as jnp
from jax import lax

D = 8192
H = 64
KVH = 8
HD = 128
FF = 14336
REQ = 32
SLOTS_DEV = 40
BLK = 256
NBLK = 128
POOL = 160
N_MEM = 4


def layout(key):
    seeds = jax.random.split(key, 4)
    quota_low = SLOTS_DEV * 3 // 4
    quota_rest = jax.random.randint(seeds[0], (N_MEM - 1,), quota_low, SLOTS_DEV + 1).astype(jnp.int32)
    quotas = jnp.concatenate([jnp.full((1,), SLOTS_DEV, jnp.int32), quota_rest])
    capacity_low = SLOTS_DEV + (N_MEM - 1) * quota_low
    long_blocks = min(NBLK, capacity_low - (REQ - 1))
    short_blocks = max(1, (capacity_low - long_blocks) // (REQ - 1))
    short_len = jax.random.randint(seeds[1], (REQ,), 1, short_blocks * BLK + 1).astype(jnp.int32)
    longest = jax.random.randint(seeds[2], (), 0, REQ)
    lengths = jnp.where(jnp.arange(REQ) == longest, long_blocks * BLK, short_len).astype(jnp.int32)
    blocks_of = (lengths + BLK - 1) // BLK
    first_block = jnp.cumsum(blocks_of) - blocks_of
    block_ids = jnp.arange(NBLK, dtype=jnp.int32)
    global_ids = first_block[:, None] + block_ids[None, :]
    is_live = block_ids[None, :] < blocks_of[:, None]
    quota_end = jnp.cumsum(quotas)
    quota_start = quota_end - quotas
    position = jnp.minimum(jnp.sum((global_ids[:, :, None] >= quota_end[None, None, :]).astype(jnp.int32), -1), N_MEM - 1)
    matches = jnp.arange(N_MEM, dtype=jnp.int32)[None, None, :] == position[:, :, None]
    order = jax.random.permutation(seeds[3], N_MEM).astype(jnp.int32)
    start_here = jnp.sum(jnp.where(matches, quota_start[None, None, :], 0), -1)
    device_of = jnp.sum(jnp.where(matches, order[None, None, :], 0), -1)
    slots = device_of * SLOTS_DEV + global_ids - start_here
    unused_fill = jnp.where(block_ids % 2 == 0, 0, N_MEM * SLOTS_DEV - 1).astype(jnp.int32)
    return (lengths, jnp.where(is_live, slots, unused_fill[None, :]).astype(jnp.int32))


def draw_lengths(key, part):
    lengths, placed = layout(key)
    return lengths


def draw_block_table(key, part):
    lengths, placed = layout(key)
    return placed


def draw_hidden_in(key, part):
    key = jax.random.fold_in(key, 11)
    seeds = jax.random.split(key, 5)
    row_scale = jnp.exp(jax.random.uniform(seeds[0], (REQ, 1), minval=math.log(0.1), maxval=math.log(1.0)))
    col_ramp = 0.5 + 0.5 * jnp.arange(D, dtype=jnp.float32) / (D - 1)
    col_scale = col_ramp * jnp.exp(jax.random.uniform(seeds[1], (D,), minval=math.log(0.8), maxval=math.log(1.25)))
    core_draw = jnp.clip(jax.random.normal(seeds[4], (REQ, D)), -3.0, 3.0)
    return (core_draw * row_scale * col_scale).astype(jnp.bfloat16)


def draw_cache_keys(key, part):
    key = jax.random.fold_in(key, 23)
    seeds = jax.random.split(key, 1)
    slot_total = N_MEM * SLOTS_DEV
    base_draw = 2.0 * jnp.clip(jax.random.normal(seeds[0], (slot_total, BLK, KVH * HD)), -6.0, 6.0)
    return base_draw.astype(jnp.bfloat16)


def levels(stream_key, extent, cuts, smallest, top_value):
    loudness, own = 1.0, jax.random.fold_in(stream_key, 6)
    for dim, parts in cuts:
        draws = jnp.exp(jax.random.uniform(jax.random.fold_in(own, dim), (parts,), jnp.float32, smallest / len(cuts), top_value / len(cuts)))
        loudness = loudness * jnp.repeat(draws, extent[dim] // parts).reshape([-1 if axis == dim else 1 for axis in range(len(extent))])
    return loudness


def gaussian(rng, extent, scale, reach, cuts=(), kind=jnp.bfloat16):
    entries = scale * jax.random.normal(rng, extent, jnp.float32)
    if cuts:
        entries = entries * levels(rng, extent, cuts, -0.22, 0.18)
    return jnp.clip(entries, -reach, reach).astype(kind)


def setup_inputs(seed: int = 0, part: int = 0) -> dict:
    key_of = jax.random.split(jax.random.key(seed), 13)
    part_splits = jax.random.split(jax.random.fold_in(key_of[12], part), 13)
    return {
        "hidden_in": draw_hidden_in(jax.random.fold_in(jax.random.fold_in(key_of[12], part), 71), part),
        "lengths": draw_lengths(jax.random.fold_in(jax.random.fold_in(key_of[12], part), 71), part),
        "block_table": draw_block_table(jax.random.fold_in(jax.random.fold_in(key_of[12], part), 71), part),
        "cache_keys": draw_cache_keys(jax.random.fold_in(jax.random.fold_in(key_of[12], part), 71), part),
        "cache_values": gaussian(part_splits[4], (POOL, BLK, KVH * HD), 1.0, 6.0, ((0, 4), (2, 4))),
        "attn_gain": jnp.clip(1.0 + 0.18 * jax.random.normal(key_of[5], (D,), jnp.float32), 0.099609375, 1.8984375).astype(jnp.bfloat16),
        "w_query": gaussian(key_of[6], (D, H * HD), D ** -0.5, 0.0625, ((0, 4), (1, 4))),
        "w_kv": gaussian(key_of[7], (D, 2, KVH * HD), D ** -0.5, 0.0625, ((0, 4), (2, 4))),
        "w_out": gaussian(key_of[8], (H * HD, D), (H * HD) ** -0.5, 0.0625, ((0, 4), (1, 4))),
        "ffn_gain": jnp.clip(1.0 + 0.18 * jax.random.normal(key_of[9], (D,), jnp.float32), 0.099609375, 1.8984375).astype(jnp.bfloat16),
        "w_gate_up": gaussian(key_of[10], (D, 2, FF), D ** -0.5, 0.0625, ((0, 4), (2, 4))),
        "w_down": gaussian(key_of[11], (FF, D), FF ** -0.5, 0.046875, ((0, 4), (1, 4))),
    }


NORM_EPS = 1e-05
ROPE_BASE = 500000.0
NEG_FILL = -1e+30

def rotate(values, positions):
    half_dim = values.shape[-1] // 2
    freq_steps = jnp.arange(half_dim, dtype=jnp.float32) * (2.0 / values.shape[-1])
    inv_freq = jnp.exp(-freq_steps * math.log(ROPE_BASE))
    angles = positions.astype(jnp.float32)[:, None, None] * inv_freq
    cosine = jnp.cos(angles)
    sine = jnp.sin(angles)
    first_half = values[..., :half_dim]
    second_half = values[..., half_dim:]
    return jnp.concatenate([first_half * cosine - second_half * sine, second_half * cosine + first_half * sine], -1)

def reference(hidden_in, lengths, block_table, cache_keys, cache_values, attn_gain, w_query, w_kv, w_out, ffn_gain, w_gate_up, w_down):
    highest = lax.Precision.HIGHEST
    scale_val = 1.0 / math.sqrt(HD)
    resid = hidden_in.astype(jnp.float32)
    attn_scale = lax.rsqrt(lax.optimization_barrier(jnp.mean(resid * resid, 1)) + NORM_EPS)
    normed = (resid * attn_gain.astype(jnp.float32)).astype(jnp.bfloat16)
    query_raw = jnp.dot(normed, w_query, preferred_element_type=jnp.float32) * attn_scale[:, None]
    kv_raw = jnp.dot(normed, w_kv.reshape(D, 2 * KVH * HD), preferred_element_type=jnp.float32) * attn_scale[:, None]
    queries = rotate(query_raw.reshape(REQ, H, HD), lengths).astype(jnp.bfloat16)
    new_keys = rotate(kv_raw[:, :KVH * HD].reshape(REQ, KVH, HD), lengths).astype(jnp.bfloat16)
    new_values = kv_raw[:, KVH * HD:].reshape(REQ, KVH, HD).astype(jnp.bfloat16)

    def one_request(inputs):
        query_row, key_new, value_new, length, table_row = inputs
        picked = table_row.astype(jnp.int32)
        key_rows = cache_keys[picked].reshape(NBLK * BLK, KVH, HD).astype(jnp.float32)
        value_rows = cache_values[picked].reshape(NBLK * BLK, KVH, HD).astype(jnp.float32)
        grouped = query_row.reshape(KVH, H // KVH, HD).astype(jnp.float32)
        scores = jnp.einsum('kgd,tkd->kgt', grouped, key_rows, precision=highest) * scale_val
        is_valid = jnp.arange(NBLK * BLK, dtype=jnp.int32) < length
        scores = jnp.where(is_valid, scores, NEG_FILL)
        own_score = jnp.einsum('kgd,kd->kg', grouped, key_new.astype(jnp.float32), precision=highest) * scale_val
        peak_val = jnp.maximum(lax.optimization_barrier(jnp.max(scores, -1)), own_score)
        weights = jnp.where(is_valid, jnp.exp(scores - peak_val[..., None]), 0.0)
        own_weight = jnp.exp(own_score - peak_val)
        rounded = lax.optimization_barrier(weights.astype(jnp.bfloat16)).astype(jnp.float32)
        numer = jnp.einsum('kgt,tkd->kgd', rounded, value_rows, precision=highest)
        numer = numer + own_weight[..., None] * value_new.astype(jnp.float32)[:, None, :]
        denom = lax.optimization_barrier(jnp.sum(weights, -1)) + own_weight
        return (numer / denom[..., None]).astype(jnp.bfloat16).reshape(H * HD)
    attended = lax.map(one_request, (queries, new_keys, new_values, lengths, block_table))
    middle = (resid + jnp.dot(attended, w_out, preferred_element_type=jnp.float32)).astype(jnp.bfloat16)
    middle_wide = middle.astype(jnp.float32)
    ffn_scale = lax.rsqrt(lax.optimization_barrier(jnp.mean(middle_wide * middle_wide, 1)) + NORM_EPS)
    normed_ffn = (middle_wide * ffn_gain.astype(jnp.float32)).astype(jnp.bfloat16)
    gate_val = jnp.dot(normed_ffn, w_gate_up[:, 0, :], preferred_element_type=jnp.float32) * ffn_scale[:, None]
    up_val = jnp.dot(normed_ffn, w_gate_up[:, 1, :], preferred_element_type=jnp.float32) * ffn_scale[:, None]
    activated = (jax.nn.silu(gate_val) * up_val).astype(jnp.bfloat16)
    updated = (middle_wide + jnp.dot(activated, w_down, preferred_element_type=jnp.float32)).astype(jnp.bfloat16)
    return (attended, updated)
```

```python
import math

import jax
import jax.numpy as jnp
from jax import lax
from jax.sharding import PartitionSpec as P

D = 8192
HD = 128
NORM_EPS = 1e-05
ROPE_BASE = 500000.0
NEG_FILL = -1e30


def to_bf16(x):
    return x.astype(jnp.bfloat16)


def shifted(x, axis, n, step):
    return lax.ppermute(x, axis, [(i, (i + step) % n) for i in range(n)])


def split_hi_lo(x):
    hi = lax.reduce_precision(x, 8, 7)
    return to_bf16(hi), to_bf16(x - hi)


def scatter_parts(x, axis, n):
    me = lax.axis_index(axis)
    parts = []
    for step in range(1, n):
        send = lax.dynamic_index_in_dim(x, (me + step) % n, 0, False)
        parts.append(shifted(send, axis, n, step))
    return parts


def gather_parts(x, axis, n):
    me = lax.axis_index(axis)
    parts = [shifted(x, axis, n, step) for step in range(n - 1, 0, -1)] + [x]
    both = jnp.concatenate(parts + parts, 0)
    rows = x.shape[0]
    return lax.dynamic_slice_in_dim(both, (n - 1 - me) * rows, n * rows, 0)


def summed(x, axis, n):
    me = lax.axis_index(axis)
    rows = x.shape[0] // n
    x = x.reshape((n, rows) + x.shape[1:])
    own = lax.dynamic_index_in_dim(x, me, 0, False)
    for part in scatter_parts(to_bf16(x), axis, n):
        own = own + part.astype(jnp.float32)
    return own


def rotary(positions, head_dim):
    half_dim = head_dim // 2
    freq_steps = jnp.arange(half_dim, dtype=jnp.float32) * (2.0 / head_dim)
    inv_freq = jnp.exp(-freq_steps * math.log(ROPE_BASE))
    angles = positions.astype(jnp.float32)[:, None, None] * inv_freq
    return jnp.cos(angles), jnp.sin(angles)


def rotate(values, cosine, sine):
    half_dim = values.shape[-1] // 2
    first_half = values[..., :half_dim]
    second_half = values[..., half_dim:]
    return jnp.concatenate(
        [first_half * cosine - second_half * sine, second_half * cosine + first_half * sine], -1
    )


def slot_stats(queries_slot, key_rows, value_rows, slot_fill, scale_val):
    scores = (
        jnp.einsum("skgd,sbkd->skgb", queries_slot, key_rows, preferred_element_type=jnp.float32)
        * scale_val
    )
    is_valid = (jnp.arange(key_rows.shape[1], dtype=jnp.int32)[None, :] < slot_fill[:, None])[
        :, None, None, :
    ]
    scores = jnp.where(is_valid, scores, NEG_FILL)
    peak_val = jnp.max(scores, -1)
    weights = jnp.where(is_valid, jnp.exp(scores - peak_val[..., None]), 0.0)
    total_w = jnp.sum(weights, -1)
    weighted = jnp.einsum(
        "skgb,sbkd->skgd",
        weights.astype(jnp.bfloat16),
        value_rows,
        preferred_element_type=jnp.float32,
    )
    return (peak_val, total_w, weighted)


def make_shards(n_mem, n_comp):
    def shards(
        hidden_in,
        lengths,
        block_table,
        cache_keys,
        cache_values,
        attn_gain,
        w_query,
        w_kv,
        w_out,
        ffn_gain,
        w_gate_up,
        w_down,
    ):
        highest = lax.Precision.HIGHEST
        req_count = hidden_in.shape[0]
        slot_count, blk_len, kv_width = cache_keys.shape
        head_dim = HD
        kv_local = kv_width // head_dim
        q_width = w_query.shape[1]
        group_size = q_width // kv_width
        scale_val = 1.0 / math.sqrt(head_dim)
        mem_pos = lax.axis_index("mem")
        rows = req_count // n_mem
        resid = hidden_in.astype(jnp.float32)
        normed = to_bf16(resid * attn_gain.astype(jnp.float32))
        query_part = jnp.dot(normed, w_query, preferred_element_type=jnp.float32)
        kv_part = jnp.dot(
            normed, w_kv.reshape(w_kv.shape[0], -1), preferred_element_type=jnp.float32
        )
        power = jnp.sum(resid * resid, 1)
        wide = jnp.concatenate(
            [query_part, kv_part, jnp.broadcast_to(power[:, None], (req_count, 128))], 1
        ).reshape(n_mem, rows, -1)
        total = lax.dynamic_index_in_dim(wide, mem_pos, 0, False)
        for part in scatter_parts(wide, "mem", n_mem):
            total = total + part
        body = q_width + 2 * kv_width
        attn_scale = lax.rsqrt(total[:, body] / D + NORM_EPS)
        cosine, sine = rotary(lengths, head_dim)
        cos_own = lax.dynamic_slice_in_dim(cosine, mem_pos * rows, rows, 0)
        sin_own = lax.dynamic_slice_in_dim(sine, mem_pos * rows, rows, 0)
        scaled = total[:, :body] * attn_scale[:, None]
        turned = rotate(
            scaled[:, : q_width + kv_width].reshape(rows, -1, head_dim), cos_own, sin_own
        ).reshape(rows, -1)
        own_qkv = to_bf16(jnp.concatenate([turned, scaled[:, q_width + kv_width :]], 1))
        qkv = gather_parts(own_qkv, "mem", n_mem)
        queries = qkv[:, :q_width].reshape(req_count, kv_local, group_size, head_dim)
        q_own = own_qkv[:, :q_width].reshape(rows, kv_local, group_size, head_dim)
        new_keys = own_qkv[:, q_width : q_width + kv_width].reshape(rows, kv_local, head_dim)
        new_values = own_qkv[:, q_width + kv_width :].reshape(rows, kv_local, head_dim)
        own_score = (
            jnp.einsum("rkgd,rkd->rkg", q_own, new_keys, preferred_element_type=jnp.float32)
            * scale_val
        )

        blk_count = block_table.shape[1]
        block_first = jnp.arange(blk_count, dtype=jnp.int32) * blk_len
        is_live = block_first[None, :] < lengths[:, None]
        local_slot = block_table - mem_pos * slot_count
        slot_ids = jnp.arange(slot_count, dtype=jnp.int32)
        owners = is_live[:, :, None] & (local_slot[:, :, None] == slot_ids[None, None, :])
        slot_member = jnp.any(owners, 1).T
        block_fill = jnp.clip(lengths[:, None] - block_first[None, :], 0, blk_len)
        slot_fill = jnp.sum(jnp.where(owners, block_fill[:, :, None], 0), (0, 1))
        queries_slot = jnp.dot(
            slot_member.astype(jnp.bfloat16),
            queries.reshape(req_count, -1),
            preferred_element_type=jnp.float32,
        )
        queries_slot = queries_slot.astype(jnp.bfloat16).reshape(
            slot_count, kv_local, group_size, head_dim
        )
        key_rows = cache_keys.reshape(slot_count, blk_len, kv_local, head_dim)
        value_rows = cache_values.reshape(slot_count, blk_len, kv_local, head_dim)
        peak_val, total_w, weighted = slot_stats(
            queries_slot, key_rows, value_rows, slot_fill, scale_val
        )
        member_mask = slot_member[:, :, None, None]
        req_peak = jnp.max(jnp.where(member_mask, peak_val[:, None], NEG_FILL), 0)
        peak_hi = lax.reduce_precision(req_peak, 8, 7)
        peak_lo = lax.reduce_precision(req_peak - peak_hi, 8, 7)
        req_peak = peak_hi + peak_lo
        slot_ref = jnp.min(jnp.where(member_mask, req_peak[None], -NEG_FILL), 1)
        factor = jnp.exp(peak_val - slot_ref)
        member_wide = slot_member.astype(jnp.float32)
        req_total = jnp.einsum("sr,skg->rkg", member_wide, total_w * factor, precision=highest)
        req_weighted = jnp.einsum(
            "sr,skgd->rkgd", member_wide, weighted * factor[..., None], precision=highest
        )
        tot_hi = lax.reduce_precision(req_total, 8, 7)
        tot_lo = req_total - tot_hi
        stats = jnp.concatenate(
            [s.reshape(req_count, -1) for s in (peak_hi, peak_lo, tot_hi, tot_lo)], 1
        )
        n_stat = kv_local * group_size
        pad = (-stats.shape[1]) % 128
        stats = jnp.pad(stats, ((0, 0), (0, pad)))
        packed = to_bf16(jnp.concatenate([req_weighted.reshape(req_count, -1), stats], 1))
        packed = packed.reshape(n_mem, rows, -1)
        pieces = [lax.dynamic_index_in_dim(packed, mem_pos, 0, False)]
        pieces += scatter_parts(packed, "mem", n_mem)
        peaks, totals, tops = [], [], []
        for piece in pieces:
            st = piece[:, q_width : q_width + 4 * n_stat].astype(jnp.float32)
            st = st.reshape(rows, 4, kv_local, group_size)
            peaks.append(st[:, 0] + st[:, 1])
            totals.append(st[:, 2] + st[:, 3])
            tops.append(
                piece[:, :q_width]
                .astype(jnp.float32)
                .reshape(rows, kv_local, group_size, head_dim)
            )
        peak = own_score
        for p in peaks:
            peak = jnp.maximum(peak, p)
        own_weight = jnp.exp(own_score - peak)
        denom = own_weight
        numer = own_weight[..., None] * new_values.astype(jnp.float32)[:, :, None, :]
        for p, t, w in zip(peaks, totals, tops):
            f = jnp.exp(p - peak)
            denom = denom + t * f
            numer = numer + w * f[..., None]
        attended_own = to_bf16(numer / denom[..., None]).reshape(rows, -1)
        attended = gather_parts(attended_own, "mem", n_mem)

        comp_pos = lax.axis_index("comp")
        rows_c = req_count // n_comp
        attn_proj = jnp.dot(attended, w_out, preferred_element_type=jnp.float32)
        resid_own = lax.dynamic_slice_in_dim(hidden_in, comp_pos * rows_c, rows_c, 0)
        middle_own = to_bf16(resid_own.astype(jnp.float32) + summed(attn_proj, "comp", n_comp))
        middle = gather_parts(middle_own, "comp", n_comp)
        middle_wide = middle.astype(jnp.float32)
        normed_ffn = to_bf16(middle_wide * ffn_gain.astype(jnp.float32))
        gate_up = jnp.einsum(
            "rd,dtf->rtf", normed_ffn, w_gate_up, preferred_element_type=jnp.float32
        ).reshape(req_count, -1)
        m_hi, m_lo = split_hi_lo(jnp.sum(middle_wide * middle_wide, 1))
        wide = jnp.concatenate(
            [
                to_bf16(gate_up),
                jnp.broadcast_to(m_hi[:, None], (req_count, 128)),
                jnp.broadcast_to(m_lo[:, None], (req_count, 128)),
            ],
            1,
        ).reshape(n_mem, rows, -1)
        total = lax.dynamic_index_in_dim(wide, mem_pos, 0, False).astype(jnp.float32)
        for part in scatter_parts(wide, "mem", n_mem):
            total = total + part.astype(jnp.float32)
        ff = w_gate_up.shape[2]
        ffn_scale = lax.rsqrt((total[:, 2 * ff] + total[:, 2 * ff + 128]) / D + NORM_EPS)
        gate = total[:, :ff] * ffn_scale[:, None]
        up = total[:, ff : 2 * ff] * ffn_scale[:, None]
        activated = gather_parts(to_bf16(jax.nn.silu(gate) * up), "mem", n_mem)
        down_part = jnp.dot(activated, w_down, preferred_element_type=jnp.float32)
        updated_own = to_bf16(middle_own.astype(jnp.float32) + summed(down_part, "comp", n_comp))
        updated = gather_parts(updated_own, "comp", n_comp)
        return (attended, updated)

    return shards


def solution(mesh):
    in_specs = (
        P("groups", "mem"),
        P("groups"),
        P("groups", None),
        P(("groups", "mem"), None, "comp"),
        P(("groups", "mem"), None, "comp"),
        P("mem"),
        P("mem", "comp"),
        P("mem", None, "comp"),
        P("comp", "mem"),
        P("mem"),
        P("mem", None, "comp"),
        P("comp", "mem"),
    )
    out_specs = (P("groups", "comp"), P("groups", "mem"))
    return jax.shard_map(
        make_shards(mesh.shape["mem"], mesh.shape["comp"]),
        mesh=mesh,
        in_specs=in_specs,
        out_specs=out_specs,
        check_vma=False,
    )
```

```python
import math

import jax
import jax.numpy as jnp
from jax import lax
from jax.experimental import pallas as pl
from jax.experimental.pallas import tpu as pltpu
from jax.sharding import PartitionSpec as P

D = 8192
HD = 128
NORM_EPS = 1e-05
ROPE_BASE = 500000.0
NEG_FILL = -1e30


def to_bf16(x):
    return x.astype(jnp.bfloat16)


def shifted(x, axis, n, step):
    return lax.ppermute(x, axis, [(i, (i + step) % n) for i in range(n)])


def split_hi_lo(x):
    hi = lax.reduce_precision(x, 8, 7)
    return to_bf16(hi), to_bf16(x - hi)


def scatter_parts(x, axis, n):
    me = lax.axis_index(axis)
    parts = []
    for step in range(1, n):
        send = lax.dynamic_index_in_dim(x, (me + step) % n, 0, False)
        parts.append(shifted(send, axis, n, step))
    return parts


def gather_parts(x, axis, n):
    me = lax.axis_index(axis)
    parts = [shifted(x, axis, n, step) for step in range(n - 1, 0, -1)] + [x]
    both = jnp.concatenate(parts + parts, 0)
    rows = x.shape[0]
    return lax.dynamic_slice_in_dim(both, (n - 1 - me) * rows, n * rows, 0)


def summed(x, axis, n):
    me = lax.axis_index(axis)
    rows = x.shape[0] // n
    x = x.reshape((n, rows) + x.shape[1:])
    own = lax.dynamic_index_in_dim(x, me, 0, False)
    for part in scatter_parts(to_bf16(x), axis, n):
        own = own + part.astype(jnp.float32)
    return own


VMEM = pltpu.VMEM
LIMIT = 12 << 20
SMALL = 2 << 20
GATE_LIMIT = 24 << 20
HIDE = (0.0, 0.0, 0.0, 0.0, 0.0, 0.0)
CUT = (6, 5)


def whole(count):
    return [pl.BlockSpec(memory_space=VMEM)] * count


def cost(hidden_us=0.0, weight=None, rows=32):
    size = 0 if weight is None else weight.size
    return pl.CostEstimate(
        flops=2 * rows * size,
        bytes_accessed=int(2 * size + hidden_us * 3e6),
        transcendentals=0,
    )


def place(parts, held, n_mem):
    me = lax.axis_index("mem")
    rows = parts[0].shape[0]
    for step, part in enumerate(parts):
        at = pl.multiple_of(lax.rem(me - step + n_mem, n_mem) * rows, rows)
        held[pl.ds(at, rows), :] = part[...].astype(jnp.float32)


def fetch(weight, start, count, after):
    pieces = 4
    step = count // pieces

    def kernel(after_ref, w_ref, out, sems):
        copies = [
            pltpu.make_async_copy(
                w_ref.at[pl.ds(start + i * step, step)], out.at[pl.ds(i * step, step)], sems.at[i]
            )
            for i in range(pieces)
        ]
        for copy in copies:
            copy.start()
        for copy in copies:
            copy.wait()

    return pl.pallas_call(
        kernel,
        in_specs=[pl.BlockSpec(memory_space=pl.ANY)] * 2,
        out_specs=pl.BlockSpec(memory_space=VMEM),
        out_shape=jax.ShapeDtypeStruct((count,) + weight.shape[1:], weight.dtype),
        scratch_shapes=[pltpu.SemaphoreType.DMA((pieces,))],
        compiler_params=pltpu.CompilerParams(vmem_limit_bytes=26 << 20),
        cost_estimate=pl.CostEstimate(
            flops=700 * count * math.prod(weight.shape[1:]),
            bytes_accessed=0,
            transcendentals=0,
        ),
    )(after, weight)


def tiled_dot(x, w_ref, out_ref, tile):
    @pl.loop(0, w_ref.shape[-1] // tile)
    def _(i):
        cols = pl.ds(pl.multiple_of(i * tile, tile), tile)
        out_ref[:, cols] = jnp.dot(
            x, w_ref[:, cols], preferred_element_type=jnp.float32
        ).astype(out_ref.dtype)


def gathered_dot(parts, weight, n_mem, keep, hidden_us):
    rows = parts[0].shape[0] * n_mem
    depth, width = weight.shape
    tile = 512 if width % 512 == 0 else 128

    def kernel(*refs):
        part_refs, w_ref = refs[:n_mem], refs[n_mem]
        outs, held = refs[n_mem + 1 : -1], refs[-1]
        place(part_refs, held, n_mem)
        x = to_bf16(held[...])
        if keep:
            outs[1][...] = x
        tiled_dot(x, w_ref, outs[0], tile)

    shapes = [jax.ShapeDtypeStruct((rows, width), jnp.bfloat16)]
    if keep:
        shapes.append(jax.ShapeDtypeStruct((rows, depth), jnp.bfloat16))
    return pl.pallas_call(
        kernel,
        in_specs=whole(n_mem + 1),
        out_specs=whole(len(shapes)),
        out_shape=shapes,
        scratch_shapes=[VMEM((rows, depth), jnp.float32)],
        compiler_params=pltpu.CompilerParams(vmem_limit_bytes=LIMIT),
        cost_estimate=cost(hidden_us, weight),
    )(*parts, weight)


def gate_up_parts(hidden, near, far, gain, held, weight, n_mem, hidden_us):
    req, depth = hidden.shape
    ff = weight.shape[2]
    rows = req // n_mem
    tile = 512 if ff % 512 == 0 else 128

    n_held = len(held)
    first = sum(h.shape[0] for h in held)
    rest = depth - first
    chunk = 128

    def kernel(hid_ref, near_ref, far_ref, gain_ref, *refs):
        held_refs, w_ref, mid_ref = refs[:n_held], refs[n_held], refs[n_held + 1]
        outs, (spread, acc, power, tail, sems) = (
            refs[n_held + 2 : n_held + 2 + n_mem],
            refs[n_held + 2 + n_mem :],
        )
        copies = [
            pltpu.make_async_copy(
                w_ref.at[pl.ds(first + i * chunk, chunk)],
                tail.at[pl.ds(i * chunk, chunk)],
                sems.at[i],
            )
            for i in range(rest // chunk)
        ]
        for copy in copies:
            copy.start()
        total = near_ref[...].astype(jnp.float32) + far_ref[...].astype(jnp.float32)
        middle = to_bf16(hid_ref[...].astype(jnp.float32) + total)
        mid_ref[...] = middle
        wide = middle.astype(jnp.float32)
        power[...] = jnp.broadcast_to(jnp.sum(wide * wide, 1, keepdims=True), power.shape)
        normed = to_bf16(wide * gain_ref[...].astype(jnp.float32))
        row = lax.broadcasted_iota(jnp.int32, (128, 256), 0)
        col = lax.broadcasted_iota(jnp.int32, (128, 256), 1)
        even = jnp.where(col == 2 * row, 1.0, 0.0).astype(jnp.bfloat16)
        odd = jnp.where(col == 2 * row + 1, 1.0, 0.0).astype(jnp.bfloat16)
        for b in range(depth // 128):
            block = normed[:, b * 128 : (b + 1) * 128]
            for half, pick in enumerate((even, odd)):
                spread[half * req : (half + 1) * req, b * 256 : (b + 1) * 256] = to_bf16(
                    jnp.dot(block, pick, preferred_element_type=jnp.float32)
                )

        def add_rows(block, at, count, fresh):
            @pl.loop(0, ff // tile)
            def _(i):
                cols = pl.ds(pl.multiple_of(i * tile, tile), tile)
                term = jnp.dot(
                    spread[:, 2 * at : 2 * (at + count)],
                    block[:, :, cols].reshape(2 * count, tile),
                    preferred_element_type=jnp.float32,
                )
                acc[:, cols] = term if fresh else acc[:, cols] + term

        at = 0
        for ref in held_refs:
            add_rows(ref, at, ref.shape[0], at == 0)
            at += ref.shape[0]
        for copy in copies:
            copy.wait()
        if rest:
            add_rows(tail, first, rest, first == 0)

        me = lax.axis_index("mem")
        for step in range(n_mem):
            at = pl.multiple_of(lax.rem(me + step, n_mem) * rows, rows)
            out = outs[step]
            gate = acc[pl.ds(at, rows), :]
            up = acc[pl.ds(at + req, rows), :]
            out[:, :ff] = to_bf16(jnp.concatenate([gate, up], 0))
            pw = power[pl.ds(at, rows), :]
            hi = to_bf16(pw).astype(jnp.float32)
            out[:, ff:] = to_bf16(jnp.concatenate([hi, pw - hi], 0))

    return pl.pallas_call(
        kernel,
        in_specs=whole(4 + n_held) + [pl.BlockSpec(memory_space=pl.ANY)],
        out_specs=whole(n_mem + 1),
        out_shape=[jax.ShapeDtypeStruct((req, depth), jnp.bfloat16)]
        + [jax.ShapeDtypeStruct((2 * rows, ff + 128), jnp.bfloat16)] * n_mem,
        scratch_shapes=[
            VMEM((2 * req, 2 * depth), jnp.bfloat16),
            VMEM((2 * req, ff), jnp.float32),
            VMEM((req, 128), jnp.float32),
            VMEM((max(rest, chunk), 2, ff), jnp.bfloat16),
            pltpu.SemaphoreType.DMA((max(rest // chunk, 1),)),
        ],
        compiler_params=pltpu.CompilerParams(vmem_limit_bytes=GATE_LIMIT),
        cost_estimate=cost(hidden_us, weight, 64),
    )(hidden, near, far, gain.reshape(1, -1), *held, weight)


def activate(parts, hidden_us):
    rows = parts[0].shape[0] // 2
    ff = parts[0].shape[1] - 128

    def kernel(*refs):
        out = refs[-1]
        total = refs[0][...].astype(jnp.float32)
        for ref in refs[1:-1]:
            total = total + ref[...].astype(jnp.float32)
        power = total[:rows, ff : ff + 1] + total[rows:, ff : ff + 1]
        scale = lax.rsqrt(power / D + NORM_EPS)
        gate = total[:rows, :ff] * scale
        up = total[rows:, :ff] * scale
        out[...] = to_bf16(gate / (1.0 + jnp.exp(-gate)) * up)

    return pl.pallas_call(
        kernel,
        in_specs=whole(len(parts)),
        out_specs=pl.BlockSpec(memory_space=VMEM),
        out_shape=jax.ShapeDtypeStruct((rows, ff), jnp.bfloat16),
        compiler_params=pltpu.CompilerParams(vmem_limit_bytes=LIMIT),
        cost_estimate=cost(hidden_us),
    )(*parts)


def around(x, axis, n):
    return [x] + [shifted(x, axis, n, step) for step in range(1, n)]


def added(left, right, hidden_us):
    def kernel(l_ref, r_ref, out):
        out[...] = to_bf16(l_ref[...].astype(jnp.float32) + r_ref[...].astype(jnp.float32))

    return pl.pallas_call(
        kernel,
        in_specs=whole(2),
        out_specs=pl.BlockSpec(memory_space=VMEM),
        out_shape=jax.ShapeDtypeStruct(left.shape, left.dtype),
        compiler_params=pltpu.CompilerParams(vmem_limit_bytes=LIMIT),
        cost_estimate=cost(hidden_us),
    )(left, right)


def pairwise(x, n, hidden_us):
    near, step = x, 1
    while True:
        far = lax.ppermute(near, "comp", [(i, i ^ step) for i in range(n)])
        step *= 2
        if step >= n:
            return near, far
        near = added(near, far, hidden_us)


def rotary(positions, head_dim):
    half_dim = head_dim // 2
    freq_steps = jnp.arange(half_dim, dtype=jnp.float32) * (2.0 / head_dim)
    inv_freq = jnp.exp(-freq_steps * math.log(ROPE_BASE))
    angles = positions.astype(jnp.float32)[:, None, None] * inv_freq
    return jnp.cos(angles), jnp.sin(angles)


def rotate(values, cosine, sine):
    half_dim = values.shape[-1] // 2
    first_half = values[..., :half_dim]
    second_half = values[..., half_dim:]
    return jnp.concatenate(
        [first_half * cosine - second_half * sine, second_half * cosine + first_half * sine], -1
    )


def slot_stats(queries_slot, key_rows, value_rows, slot_fill, scale_val):
    scores = (
        jnp.einsum("skgd,sbkd->skgb", queries_slot, key_rows, preferred_element_type=jnp.float32)
        * scale_val
    )
    is_valid = (jnp.arange(key_rows.shape[1], dtype=jnp.int32)[None, :] < slot_fill[:, None])[
        :, None, None, :
    ]
    scores = jnp.where(is_valid, scores, NEG_FILL)
    peak_val = jnp.max(scores, -1)
    weights = jnp.where(is_valid, jnp.exp(scores - peak_val[..., None]), 0.0)
    total_w = jnp.sum(weights, -1)
    weighted = jnp.einsum(
        "skgb,sbkd->skgd",
        weights.astype(jnp.bfloat16),
        value_rows,
        preferred_element_type=jnp.float32,
    )
    return (peak_val, total_w, weighted)


def make_shards(n_mem, n_comp):
    def shards(
        hidden_in,
        lengths,
        block_table,
        cache_keys,
        cache_values,
        attn_gain,
        w_query,
        w_kv,
        w_out,
        ffn_gain,
        w_gate_up,
        w_down,
    ):
        highest = lax.Precision.HIGHEST
        req_count = hidden_in.shape[0]
        slot_count, blk_len, kv_width = cache_keys.shape
        head_dim = HD
        kv_local = kv_width // head_dim
        q_width = w_query.shape[1]
        group_size = q_width // kv_width
        scale_val = 1.0 / math.sqrt(head_dim)
        mem_pos = lax.axis_index("mem")
        rows = req_count // n_mem
        resid = hidden_in.astype(jnp.float32)
        normed = to_bf16(resid * attn_gain.astype(jnp.float32))
        query_part = jnp.dot(normed, w_query, preferred_element_type=jnp.float32)
        kv_part = jnp.dot(
            normed, w_kv.reshape(w_kv.shape[0], -1), preferred_element_type=jnp.float32
        )
        power = jnp.sum(resid * resid, 1)
        wide = jnp.concatenate(
            [query_part, kv_part, jnp.broadcast_to(power[:, None], (req_count, 128))], 1
        ).reshape(n_mem, rows, -1)
        total = lax.dynamic_index_in_dim(wide, mem_pos, 0, False)
        for part in scatter_parts(wide, "mem", n_mem):
            total = total + part
        body = q_width + 2 * kv_width
        attn_scale = lax.rsqrt(total[:, body] / D + NORM_EPS)
        cosine, sine = rotary(lengths, head_dim)
        cos_own = lax.dynamic_slice_in_dim(cosine, mem_pos * rows, rows, 0)
        sin_own = lax.dynamic_slice_in_dim(sine, mem_pos * rows, rows, 0)
        scaled = total[:, :body] * attn_scale[:, None]
        turned = rotate(
            scaled[:, : q_width + kv_width].reshape(rows, -1, head_dim), cos_own, sin_own
        ).reshape(rows, -1)
        own_qkv = to_bf16(jnp.concatenate([turned, scaled[:, q_width + kv_width :]], 1))
        qkv = gather_parts(own_qkv, "mem", n_mem)
        queries = qkv[:, :q_width].reshape(req_count, kv_local, group_size, head_dim)
        q_own = own_qkv[:, :q_width].reshape(rows, kv_local, group_size, head_dim)
        new_keys = own_qkv[:, q_width : q_width + kv_width].reshape(rows, kv_local, head_dim)
        new_values = own_qkv[:, q_width + kv_width :].reshape(rows, kv_local, head_dim)
        own_score = (
            jnp.einsum("rkgd,rkd->rkg", q_own, new_keys, preferred_element_type=jnp.float32)
            * scale_val
        )

        blk_count = block_table.shape[1]
        block_first = jnp.arange(blk_count, dtype=jnp.int32) * blk_len
        is_live = block_first[None, :] < lengths[:, None]
        local_slot = block_table - mem_pos * slot_count
        slot_ids = jnp.arange(slot_count, dtype=jnp.int32)
        owners = is_live[:, :, None] & (local_slot[:, :, None] == slot_ids[None, None, :])
        slot_member = jnp.any(owners, 1).T
        block_fill = jnp.clip(lengths[:, None] - block_first[None, :], 0, blk_len)
        slot_fill = jnp.sum(jnp.where(owners, block_fill[:, :, None], 0), (0, 1))
        queries_slot = jnp.dot(
            slot_member.astype(jnp.bfloat16),
            queries.reshape(req_count, -1),
            preferred_element_type=jnp.float32,
        )
        queries_slot = queries_slot.astype(jnp.bfloat16).reshape(
            slot_count, kv_local, group_size, head_dim
        )
        key_rows = cache_keys.reshape(slot_count, blk_len, kv_local, head_dim)
        value_rows = cache_values.reshape(slot_count, blk_len, kv_local, head_dim)
        peak_val, total_w, weighted = slot_stats(
            queries_slot, key_rows, value_rows, slot_fill, scale_val
        )
        member_mask = slot_member[:, :, None, None]
        req_peak = jnp.max(jnp.where(member_mask, peak_val[:, None], NEG_FILL), 0)
        peak_hi = lax.reduce_precision(req_peak, 8, 7)
        peak_lo = lax.reduce_precision(req_peak - peak_hi, 8, 7)
        req_peak = peak_hi + peak_lo
        slot_ref = jnp.min(jnp.where(member_mask, req_peak[None], -NEG_FILL), 1)
        factor = jnp.exp(peak_val - slot_ref)
        member_wide = slot_member.astype(jnp.float32)
        req_total = jnp.einsum("sr,skg->rkg", member_wide, total_w * factor, precision=highest)
        req_weighted = jnp.einsum(
            "sr,skgd->rkgd", member_wide, weighted * factor[..., None], precision=highest
        )
        tot_hi = lax.reduce_precision(req_total, 8, 7)
        tot_lo = req_total - tot_hi
        stats = jnp.concatenate(
            [s.reshape(req_count, -1) for s in (peak_hi, peak_lo, tot_hi, tot_lo)], 1
        )
        n_stat = kv_local * group_size
        pad = (-stats.shape[1]) % 128
        stats = jnp.pad(stats, ((0, 0), (0, pad)))
        packed = to_bf16(jnp.concatenate([req_weighted.reshape(req_count, -1), stats], 1))
        packed = packed.reshape(n_mem, rows, -1)
        pieces = [lax.dynamic_index_in_dim(packed, mem_pos, 0, False)]
        pieces += scatter_parts(packed, "mem", n_mem)
        peaks, totals, tops = [], [], []
        for piece in pieces:
            st = piece[:, q_width : q_width + 4 * n_stat].astype(jnp.float32)
            st = st.reshape(rows, 4, kv_local, group_size)
            peaks.append(st[:, 0] + st[:, 1])
            totals.append(st[:, 2] + st[:, 3])
            tops.append(
                piece[:, :q_width]
                .astype(jnp.float32)
                .reshape(rows, kv_local, group_size, head_dim)
            )
        peak = own_score
        for p in peaks:
            peak = jnp.maximum(peak, p)
        own_weight = jnp.exp(own_score - peak)
        denom = own_weight
        numer = own_weight[..., None] * new_values.astype(jnp.float32)[:, :, None, :]
        for p, t, w in zip(peaks, totals, tops):
            f = jnp.exp(p - peak)
            denom = denom + t * f
            numer = numer + w * f[..., None]
        attended_own = to_bf16(numer / denom[..., None]).reshape(rows, -1)
        if rows % 8:
            attended = gather_parts(attended_own, "mem", n_mem)

            comp_pos = lax.axis_index("comp")
            rows_c = req_count // n_comp
            attn_proj = jnp.dot(attended, w_out, preferred_element_type=jnp.float32)
            resid_own = lax.dynamic_slice_in_dim(hidden_in, comp_pos * rows_c, rows_c, 0)
            middle_own = to_bf16(resid_own.astype(jnp.float32) + summed(attn_proj, "comp", n_comp))
            middle = gather_parts(middle_own, "comp", n_comp)
            middle_wide = middle.astype(jnp.float32)
            normed_ffn = to_bf16(middle_wide * ffn_gain.astype(jnp.float32))
            gate_up = jnp.einsum(
                "rd,dtf->rtf", normed_ffn, w_gate_up, preferred_element_type=jnp.float32
            ).reshape(req_count, -1)
            m_hi, m_lo = split_hi_lo(jnp.sum(middle_wide * middle_wide, 1))
            wide = jnp.concatenate(
                [
                    to_bf16(gate_up),
                    jnp.broadcast_to(m_hi[:, None], (req_count, 128)),
                    jnp.broadcast_to(m_lo[:, None], (req_count, 128)),
                ],
                1,
            ).reshape(n_mem, rows, -1)
            total = lax.dynamic_index_in_dim(wide, mem_pos, 0, False).astype(jnp.float32)
            for part in scatter_parts(wide, "mem", n_mem):
                total = total + part.astype(jnp.float32)
            ff = w_gate_up.shape[2]
            ffn_scale = lax.rsqrt((total[:, 2 * ff] + total[:, 2 * ff + 128]) / D + NORM_EPS)
            gate = total[:, :ff] * ffn_scale[:, None]
            up = total[:, ff : 2 * ff] * ffn_scale[:, None]
            activated = gather_parts(to_bf16(jax.nn.silu(gate) * up), "mem", n_mem)
            down_part = jnp.dot(activated, w_down, preferred_element_type=jnp.float32)
            updated_own = to_bf16(middle_own.astype(jnp.float32) + summed(down_part, "comp", n_comp))
            updated = gather_parts(updated_own, "comp", n_comp)
            return (attended, updated)

        depth = w_gate_up.shape[0]
        cut_a, cut_b = depth * CUT[0] // 16, depth * CUT[1] // 16
        out_held = fetch(w_out, 0, w_out.shape[0], own_qkv)
        gate_a = fetch(w_gate_up, 0, cut_a, attended_own)
        proj, attended = gathered_dot(
            around(attended_own, "mem", n_mem), out_held, n_mem, True, HIDE[2]
        )
        near, far = pairwise(proj, n_comp, HIDE[3])
        gate_b = fetch(w_gate_up, cut_a, cut_b, near)
        middle, *terms = gate_up_parts(
            hidden_in, near, far, ffn_gain, (gate_a, gate_b), w_gate_up, n_mem, HIDE[3]
        )
        down_held = fetch(w_down, 0, w_down.shape[0], terms[0])
        terms = terms[:1] + [shifted(t, "mem", n_mem, s) for s, t in enumerate(terms) if s]
        activated = activate(terms, HIDE[4])
        (down,) = gathered_dot(
            around(activated, "mem", n_mem), down_held, n_mem, False, HIDE[5]
        )
        near, far = pairwise(down, n_comp, 0.0)
        updated = to_bf16(
            middle.astype(jnp.float32) + (near.astype(jnp.float32) + far.astype(jnp.float32))
        )
        return (attended, updated)

    return shards


def solution(mesh):
    in_specs = (
        P("groups", "mem"),
        P("groups"),
        P("groups", None),
        P(("groups", "mem"), None, "comp"),
        P(("groups", "mem"), None, "comp"),
        P("mem"),
        P("mem", "comp"),
        P("mem", None, "comp"),
        P("comp", "mem"),
        P("mem"),
        P("mem", None, "comp"),
        P("comp", "mem"),
    )
    out_specs = (P("groups", "comp"), P("groups", "mem"))
    return jax.shard_map(
        make_shards(mesh.shape["mem"], mesh.shape["comp"]),
        mesh=mesh,
        in_specs=in_specs,
        out_specs=out_specs,
        check_vma=False,
    )
```

```python
import math

import jax
import jax.numpy as jnp
from jax import lax
from jax.experimental import pallas as pl
from jax.experimental.pallas import tpu as pltpu
from jax.sharding import PartitionSpec as P

D = 8192
HD = 128
NORM_EPS = 1e-05
ROPE_BASE = 500000.0
NEG_FILL = -1e30


def to_bf16(x):
    return x.astype(jnp.bfloat16)


def shifted(x, axis, n, step):
    return lax.ppermute(x, axis, [(i, (i + step) % n) for i in range(n)])


def split_hi_lo(x):
    hi = lax.reduce_precision(x, 8, 7)
    return to_bf16(hi), to_bf16(x - hi)


def scatter_parts(x, axis, n):
    me = lax.axis_index(axis)
    parts = []
    for step in range(1, n):
        send = lax.dynamic_index_in_dim(x, (me + step) % n, 0, False)
        parts.append(shifted(send, axis, n, step))
    return parts


def gather_parts(x, axis, n):
    me = lax.axis_index(axis)
    parts = [shifted(x, axis, n, step) for step in range(n - 1, 0, -1)] + [x]
    both = jnp.concatenate(parts + parts, 0)
    rows = x.shape[0]
    return lax.dynamic_slice_in_dim(both, (n - 1 - me) * rows, n * rows, 0)


def summed(x, axis, n):
    me = lax.axis_index(axis)
    rows = x.shape[0] // n
    x = x.reshape((n, rows) + x.shape[1:])
    own = lax.dynamic_index_in_dim(x, me, 0, False)
    for part in scatter_parts(to_bf16(x), axis, n):
        own = own + part.astype(jnp.float32)
    return own


VMEM = pltpu.VMEM
LIMIT = 12 << 20
GATE_LIMIT = 24 << 20
QUERY_LIMIT = 56 << 20
FETCH_LIMIT = 26 << 20
CUT = (6, 5)
OUT_LIMIT = 40 << 20


def whole(count):
    return [pl.BlockSpec(memory_space=VMEM)] * count


def cost(hidden_us=0.0, weight=None, rows=32):
    size = 0 if weight is None else weight.size
    return pl.CostEstimate(
        flops=2 * rows * size,
        bytes_accessed=int(2 * size + hidden_us * 3e6),
        transcendentals=0,
    )


def place(parts, held, n_mem):
    me = lax.axis_index("mem")
    rows = parts[0].shape[0]
    for step, part in enumerate(parts):
        at = pl.multiple_of(lax.rem(me - step + n_mem, n_mem) * rows, rows)
        held[pl.ds(at, rows), :] = part[...].astype(jnp.float32)


def fetch(weight, start, count, after, limit=None):
    pieces = 4
    step = count // pieces

    def kernel(after_ref, w_ref, out, sems):
        copies = [
            pltpu.make_async_copy(
                w_ref.at[pl.ds(start + i * step, step)], out.at[pl.ds(i * step, step)], sems.at[i]
            )
            for i in range(pieces)
        ]
        for copy in copies:
            copy.start()
        for copy in copies:
            copy.wait()

    return pl.pallas_call(
        kernel,
        in_specs=[pl.BlockSpec(memory_space=pl.ANY)] * 2,
        out_specs=pl.BlockSpec(memory_space=VMEM),
        out_shape=jax.ShapeDtypeStruct((count,) + weight.shape[1:], weight.dtype),
        scratch_shapes=[pltpu.SemaphoreType.DMA((pieces,))],
        compiler_params=pltpu.CompilerParams(vmem_limit_bytes=FETCH_LIMIT if limit is None else limit),
        cost_estimate=pl.CostEstimate(
            flops=700 * count * math.prod(weight.shape[1:]),
            bytes_accessed=0,
            transcendentals=0,
        ),
    )(after, weight)


def tiled_dot(x, w_ref, out_ref, tile):
    @pl.loop(0, w_ref.shape[-1] // tile)
    def _(i):
        cols = pl.ds(pl.multiple_of(i * tile, tile), tile)
        out_ref[:, cols] = jnp.dot(
            x, w_ref[:, cols], preferred_element_type=jnp.float32
        ).astype(out_ref.dtype)


def gathered_dot(parts, weight, n_mem, keep, beside=()):
    rows = parts[0].shape[0] * n_mem
    depth, width = weight.shape
    tile = 512 if width % 512 == 0 else 128

    def kernel(*refs):
        part_refs, w_ref = refs[:n_mem], refs[n_mem]
        outs, held = refs[n_mem + 1 + len(beside) : -1], refs[-1]
        place(part_refs, held, n_mem)
        x = to_bf16(held[...])
        if keep:
            outs[1][...] = x
        tiled_dot(x, w_ref, outs[0], tile)

    shapes = [jax.ShapeDtypeStruct((rows, width), jnp.bfloat16)]
    if keep:
        shapes.append(jax.ShapeDtypeStruct((rows, depth), jnp.bfloat16))
    return pl.pallas_call(
        kernel,
        in_specs=whole(n_mem + 1) + [pl.BlockSpec(memory_space=pl.ANY)] * len(beside),
        out_specs=whole(len(shapes)),
        out_shape=shapes,
        scratch_shapes=[VMEM((rows, depth), jnp.float32)],
        compiler_params=pltpu.CompilerParams(vmem_limit_bytes=LIMIT),
        cost_estimate=cost(0.0, weight),
    )(*parts, weight, *beside)


def unfold(x, spread):
    count = x.shape[0]
    row = lax.broadcasted_iota(jnp.int32, (128, 256), 0)
    col = lax.broadcasted_iota(jnp.int32, (128, 256), 1)
    even = jnp.where(col == 2 * row, 1.0, 0.0).astype(jnp.bfloat16)
    odd = jnp.where(col == 2 * row + 1, 1.0, 0.0).astype(jnp.bfloat16)
    for b in range(x.shape[1] // 128):
        block = x[:, b * 128 : (b + 1) * 128]
        for half, pick in enumerate((even, odd)):
            spread[half * count : (half + 1) * count, b * 256 : (b + 1) * 256] = to_bf16(
                jnp.dot(block, pick, preferred_element_type=jnp.float32)
            )


def query_parts(hidden, gain, w_query, w_kv, n_mem):
    req, depth = hidden.shape
    q_width, kv_width = w_query.shape[1], w_kv.shape[2]
    rows = req // n_mem
    body = q_width + 2 * kv_width
    chunks, ahead = 8, 3
    step = depth // chunks

    def kernel(hid_ref, gain_ref, wq_ref, wkv_ref, *refs):
        outs = refs[:n_mem]
        acc, spread, q_buf, kv_buf, q_sems, kv_sems, hid_buf, gain_buf = refs[n_mem:]
        small = [
            pltpu.make_async_copy(hid_ref, hid_buf, kv_sems.at[1]),
            pltpu.make_async_copy(gain_ref, gain_buf, kv_sems.at[2]),
        ]
        for copy in small:
            copy.start()
        kv_copy = pltpu.make_async_copy(wkv_ref, kv_buf, kv_sems.at[0])
        kv_copy.start()
        copies = [
            pltpu.make_async_copy(
                wq_ref.at[pl.ds(i * step, step)], q_buf.at[pl.ds(i * step, step)], q_sems.at[i]
            )
            for i in range(chunks)
        ]
        for copy in copies[:ahead]:
            copy.start()
        for copy in small:
            copy.wait()
        wide = hid_buf[...].astype(jnp.float32)
        acc[:, body:] = jnp.broadcast_to(jnp.sum(wide * wide, 1, keepdims=True), (req, 128))
        normed = to_bf16(wide * gain_buf[...].astype(jnp.float32).reshape(1, depth))
        unfold(normed, spread)
        kv_copy.wait()
        both = jnp.dot(
            spread[...],
            kv_buf[...].reshape(2 * depth, kv_width),
            preferred_element_type=jnp.float32,
        )
        acc[:, q_width : q_width + kv_width] = both[:req]
        acc[:, q_width + kv_width : body] = both[req:]
        for i, copy in enumerate(copies):
            copy.wait()
            if i + ahead < chunks:
                copies[i + ahead].start()
            term = jnp.dot(
                normed[:, i * step : (i + 1) * step],
                q_buf[i * step : (i + 1) * step, :],
                preferred_element_type=jnp.float32,
            )
            acc[:, :q_width] = term if i == 0 else acc[:, :q_width] + term
        me = lax.axis_index("mem")
        for step_to in range(n_mem):
            at = pl.multiple_of(lax.rem(me + step_to, n_mem) * rows, rows)
            outs[step_to][...] = acc[pl.ds(at, rows), :]

    return pl.pallas_call(
        kernel,
        in_specs=[pl.BlockSpec(memory_space=pltpu.HBM)] * 4,
        out_specs=whole(n_mem),
        out_shape=[jax.ShapeDtypeStruct((rows, body + 128), jnp.float32)] * n_mem,
        scratch_shapes=[
            VMEM((req, body + 128), jnp.float32),
            VMEM((2 * req, 2 * depth), jnp.bfloat16),
            VMEM(w_query.shape, jnp.bfloat16),
            VMEM(w_kv.shape, jnp.bfloat16),
            pltpu.SemaphoreType.DMA((chunks,)),
            pltpu.SemaphoreType.DMA((3,)),
            VMEM(hidden.shape, jnp.bfloat16),
            VMEM(gain.shape, jnp.bfloat16),
        ],
        compiler_params=pltpu.CompilerParams(vmem_limit_bytes=QUERY_LIMIT),
        cost_estimate=pl.CostEstimate(
            flops=2 * req * w_query.size, bytes_accessed=2 * w_query.size, transcendentals=0
        ),
    )(hidden, gain, w_query, w_kv)


def turned_parts(parts, cosine, sine, q_width, kv_width, beside):
    rows = parts[0].shape[0]
    body = q_width + 2 * kv_width
    n = len(parts)

    def kernel(*refs):
        cos_ref, sin_ref, out = refs[n], refs[n + 1], refs[-1]
        total = refs[0][...]
        for ref in refs[1:n]:
            total = total + ref[...]
        scale = lax.rsqrt(total[:, body : body + 1] / D + NORM_EPS)
        cos, sin = cos_ref[...], sin_ref[...]
        for at in range(0, q_width + kv_width, HD):
            head = total[:, at : at + HD] * scale
            out[:, at : at + HD] = to_bf16(head * cos + pltpu.roll(head, HD // 2, 1) * sin)
        out[:, q_width + kv_width :] = to_bf16(total[:, q_width + kv_width : body] * scale)

    return pl.pallas_call(
        kernel,
        in_specs=whole(n + 2) + [pl.BlockSpec(memory_space=pl.ANY)] * len(beside),
        out_specs=pl.BlockSpec(memory_space=VMEM),
        out_shape=jax.ShapeDtypeStruct((rows, body), jnp.bfloat16),
        compiler_params=pltpu.CompilerParams(vmem_limit_bytes=LIMIT),
        cost_estimate=cost(0.0),
    )(*parts, cosine, sine, *beside)


def gate_up_parts(hidden, near, far, gain, held, weight, n_mem, hidden_us):
    req, depth = hidden.shape
    ff = weight.shape[2]
    rows = req // n_mem
    tile = ff // 2 if ff % 256 == 0 else 128

    n_held = len(held)
    first = sum(h.shape[0] for h in held)
    rest = depth - first
    chunk = 128

    def kernel(hid_ref, near_ref, far_ref, gain_ref, *refs):
        held_refs, w_ref, mid_ref = refs[:n_held], refs[n_held], refs[n_held + 1]
        outs, (spread, acc, power, tail, sems) = (
            refs[n_held + 2 : n_held + 2 + n_mem],
            refs[n_held + 2 + n_mem :],
        )
        copies = [
            pltpu.make_async_copy(
                w_ref.at[pl.ds(first + i * chunk, chunk)],
                tail.at[pl.ds(i * chunk, chunk)],
                sems.at[i],
            )
            for i in range(rest // chunk)
        ]
        for copy in copies:
            copy.start()
        total = near_ref[...].astype(jnp.float32) + far_ref[...].astype(jnp.float32)
        middle = to_bf16(hid_ref[...].astype(jnp.float32) + total)
        mid_ref[...] = middle
        wide = middle.astype(jnp.float32)
        power[...] = jnp.broadcast_to(jnp.sum(wide * wide, 1, keepdims=True), power.shape)
        normed = to_bf16(wide * gain_ref[...].astype(jnp.float32).reshape(1, depth))
        unfold(normed, spread)

        def add_rows(block, at, count, fresh):
            @pl.loop(0, ff // tile)
            def _(i):
                cols = pl.ds(pl.multiple_of(i * tile, tile), tile)
                term = jnp.dot(
                    spread[:, 2 * at : 2 * (at + count)],
                    block[:, :, cols].reshape(2 * count, tile),
                    preferred_element_type=jnp.float32,
                )
                acc[:, cols] = term if fresh else acc[:, cols] + term

        at = 0
        for ref in held_refs:
            add_rows(ref, at, ref.shape[0], at == 0)
            at += ref.shape[0]
        for copy in copies:
            copy.wait()
        if rest:
            add_rows(tail, first, rest, first == 0)

        me = lax.axis_index("mem")
        for step in range(n_mem):
            at = pl.multiple_of(lax.rem(me + step, n_mem) * rows, rows)
            out = outs[step]
            gate = acc[pl.ds(at, rows), :]
            up = acc[pl.ds(at + req, rows), :]
            out[:, :ff] = to_bf16(jnp.concatenate([gate, up], 0))
            pw = power[pl.ds(at, rows), :]
            hi = to_bf16(pw).astype(jnp.float32)
            out[:, ff:] = to_bf16(jnp.concatenate([hi, pw - hi], 0))

    return pl.pallas_call(
        kernel,
        in_specs=whole(4 + n_held) + [pl.BlockSpec(memory_space=pl.ANY)],
        out_specs=whole(n_mem + 1),
        out_shape=[jax.ShapeDtypeStruct((req, depth), jnp.bfloat16)]
        + [jax.ShapeDtypeStruct((2 * rows, ff + 128), jnp.bfloat16)] * n_mem,
        scratch_shapes=[
            VMEM((2 * req, 2 * depth), jnp.bfloat16),
            VMEM((2 * req, ff), jnp.float32),
            VMEM((req, 128), jnp.float32),
            VMEM((max(rest, chunk), 2, ff), jnp.bfloat16),
            pltpu.SemaphoreType.DMA((max(rest // chunk, 1),)),
        ],
        compiler_params=pltpu.CompilerParams(vmem_limit_bytes=GATE_LIMIT),
        cost_estimate=cost(hidden_us, weight, 64),
    )(hidden, near, far, gain, *held, weight)


def activate(parts, beside):
    rows = parts[0].shape[0] // 2
    ff = parts[0].shape[1] - 128

    def kernel(*refs):
        out = refs[-1]
        total = refs[0][...].astype(jnp.float32)
        for ref in refs[1 : len(parts)]:
            total = total + ref[...].astype(jnp.float32)
        power = total[:rows, ff : ff + 1] + total[rows:, ff : ff + 1]
        scale = lax.rsqrt(power / D + NORM_EPS)
        gate = total[:rows, :ff] * scale
        up = total[rows:, :ff] * scale
        out[...] = to_bf16(gate / (1.0 + jnp.exp(-gate)) * up)

    return pl.pallas_call(
        kernel,
        in_specs=whole(len(parts)) + [pl.BlockSpec(memory_space=pl.ANY)] * len(beside),
        out_specs=pl.BlockSpec(memory_space=VMEM),
        out_shape=jax.ShapeDtypeStruct((rows, ff), jnp.bfloat16),
        compiler_params=pltpu.CompilerParams(vmem_limit_bytes=LIMIT),
        cost_estimate=cost(0.0),
    )(*parts, *beside)


def around(x, axis, n):
    return [x] + [shifted(x, axis, n, step) for step in range(1, n)]


def added(left, right, hidden_us):
    def kernel(l_ref, r_ref, out):
        out[...] = to_bf16(l_ref[...].astype(jnp.float32) + r_ref[...].astype(jnp.float32))

    return pl.pallas_call(
        kernel,
        in_specs=whole(2),
        out_specs=pl.BlockSpec(memory_space=VMEM),
        out_shape=jax.ShapeDtypeStruct(left.shape, left.dtype),
        compiler_params=pltpu.CompilerParams(vmem_limit_bytes=LIMIT),
        cost_estimate=cost(hidden_us),
    )(left, right)


def pairwise(x, n, hidden_us):
    near, step = x, 1
    while True:
        far = lax.ppermute(near, "comp", [(i, i ^ step) for i in range(n)])
        step *= 2
        if step >= n:
            return near, far
        near = added(near, far, hidden_us)


def rotary(positions, head_dim):
    half_dim = head_dim // 2
    freq_steps = jnp.arange(half_dim, dtype=jnp.float32) * (2.0 / head_dim)
    inv_freq = jnp.exp(-freq_steps * math.log(ROPE_BASE))
    angles = positions.astype(jnp.float32)[:, None, None] * inv_freq
    return jnp.cos(angles), jnp.sin(angles)


def rotate(values, cosine, sine):
    half_dim = values.shape[-1] // 2
    first_half = values[..., :half_dim]
    second_half = values[..., half_dim:]
    return jnp.concatenate(
        [first_half * cosine - second_half * sine, second_half * cosine + first_half * sine], -1
    )


def slot_stats(queries_slot, key_rows, value_rows, slot_fill, scale_val):
    scores = (
        jnp.einsum("skgd,sbkd->skgb", queries_slot, key_rows, preferred_element_type=jnp.float32)
        * scale_val
    )
    is_valid = (jnp.arange(key_rows.shape[1], dtype=jnp.int32)[None, :] < slot_fill[:, None])[
        :, None, None, :
    ]
    scores = jnp.where(is_valid, scores, NEG_FILL)
    peak_val = jnp.max(scores, -1)
    weights = jnp.where(is_valid, jnp.exp(scores - peak_val[..., None]), 0.0)
    total_w = jnp.sum(weights, -1)
    weighted = jnp.einsum(
        "skgb,sbkd->skgd",
        weights.astype(jnp.bfloat16),
        value_rows,
        preferred_element_type=jnp.float32,
    )
    return (peak_val, total_w, weighted)


def make_shards(n_mem, n_comp):
    def shards(
        hidden_in,
        lengths,
        block_table,
        cache_keys,
        cache_values,
        attn_gain,
        w_query,
        w_kv,
        w_out,
        ffn_gain,
        w_gate_up,
        w_down,
    ):
        highest = lax.Precision.HIGHEST
        req_count = hidden_in.shape[0]
        slot_count, blk_len, kv_width = cache_keys.shape
        head_dim = HD
        kv_local = kv_width // head_dim
        q_width = w_query.shape[1]
        group_size = q_width // kv_width
        scale_val = 1.0 / math.sqrt(head_dim)
        mem_pos = lax.axis_index("mem")
        rows = req_count // n_mem
        if rows % 8:
            resid = hidden_in.astype(jnp.float32)
            normed = to_bf16(resid * attn_gain.astype(jnp.float32))
            query_part = jnp.dot(normed, w_query, preferred_element_type=jnp.float32)
            kv_part = jnp.dot(
                normed, w_kv.reshape(w_kv.shape[0], -1), preferred_element_type=jnp.float32
            )
            power = jnp.sum(resid * resid, 1)
            wide = jnp.concatenate(
                [query_part, kv_part, jnp.broadcast_to(power[:, None], (req_count, 128))], 1
            ).reshape(n_mem, rows, -1)
            total = lax.dynamic_index_in_dim(wide, mem_pos, 0, False)
            for part in scatter_parts(wide, "mem", n_mem):
                total = total + part
            body = q_width + 2 * kv_width
            attn_scale = lax.rsqrt(total[:, body] / D + NORM_EPS)
            cosine, sine = rotary(lengths, head_dim)
            cos_own = lax.dynamic_slice_in_dim(cosine, mem_pos * rows, rows, 0)
            sin_own = lax.dynamic_slice_in_dim(sine, mem_pos * rows, rows, 0)
            scaled = total[:, :body] * attn_scale[:, None]
            turned = rotate(
                scaled[:, : q_width + kv_width].reshape(rows, -1, head_dim), cos_own, sin_own
            ).reshape(rows, -1)
            own_qkv = to_bf16(jnp.concatenate([turned, scaled[:, q_width + kv_width :]], 1))
        else:
            here = lax.dynamic_slice_in_dim(lengths, mem_pos * rows, rows, 0)
            cosine, sine = rotary(here, head_dim)
            cosine = jnp.concatenate([cosine, cosine], -1)[:, 0]
            sine = jnp.concatenate([-sine, sine], -1)[:, 0]
            terms = list(query_parts(hidden_in, attn_gain, w_query, w_kv, n_mem))
            out_held = fetch(w_out, 0, w_out.shape[0], terms[0], OUT_LIMIT)
            terms = terms[:1] + [shifted(t, "mem", n_mem, s) for s, t in enumerate(terms) if s]
            own_qkv = turned_parts(terms, cosine, sine, q_width, kv_width, (out_held,))
        qkv = gather_parts(own_qkv, "mem", n_mem)
        queries = qkv[:, :q_width].reshape(req_count, kv_local, group_size, head_dim)
        q_own = own_qkv[:, :q_width].reshape(rows, kv_local, group_size, head_dim)
        new_keys = own_qkv[:, q_width : q_width + kv_width].reshape(rows, kv_local, head_dim)
        new_values = own_qkv[:, q_width + kv_width :].reshape(rows, kv_local, head_dim)
        own_score = (
            jnp.einsum("rkgd,rkd->rkg", q_own, new_keys, preferred_element_type=jnp.float32)
            * scale_val
        )

        blk_count = block_table.shape[1]
        block_first = jnp.arange(blk_count, dtype=jnp.int32) * blk_len
        is_live = block_first[None, :] < lengths[:, None]
        local_slot = block_table - mem_pos * slot_count
        slot_ids = jnp.arange(slot_count, dtype=jnp.int32)
        owners = is_live[:, :, None] & (local_slot[:, :, None] == slot_ids[None, None, :])
        slot_member = jnp.any(owners, 1).T
        block_fill = jnp.clip(lengths[:, None] - block_first[None, :], 0, blk_len)
        slot_fill = jnp.sum(jnp.where(owners, block_fill[:, :, None], 0), (0, 1))
        queries_slot = jnp.dot(
            slot_member.astype(jnp.bfloat16),
            queries.reshape(req_count, -1),
            preferred_element_type=jnp.float32,
        )
        queries_slot = queries_slot.astype(jnp.bfloat16).reshape(
            slot_count, kv_local, group_size, head_dim
        )
        key_rows = cache_keys.reshape(slot_count, blk_len, kv_local, head_dim)
        value_rows = cache_values.reshape(slot_count, blk_len, kv_local, head_dim)
        peak_val, total_w, weighted = slot_stats(
            queries_slot, key_rows, value_rows, slot_fill, scale_val
        )
        member_mask = slot_member[:, :, None, None]
        req_peak = jnp.max(jnp.where(member_mask, peak_val[:, None], NEG_FILL), 0)
        peak_hi = lax.reduce_precision(req_peak, 8, 7)
        peak_lo = lax.reduce_precision(req_peak - peak_hi, 8, 7)
        req_peak = peak_hi + peak_lo
        slot_ref = jnp.min(jnp.where(member_mask, req_peak[None], -NEG_FILL), 1)
        factor = jnp.exp(peak_val - slot_ref)
        member_wide = slot_member.astype(jnp.float32)
        req_total = jnp.einsum("sr,skg->rkg", member_wide, total_w * factor, precision=highest)
        req_weighted = jnp.einsum(
            "sr,skgd->rkgd", member_wide, weighted * factor[..., None], precision=highest
        )
        tot_hi = lax.reduce_precision(req_total, 8, 7)
        tot_lo = req_total - tot_hi
        stats = jnp.concatenate(
            [s.reshape(req_count, -1) for s in (peak_hi, peak_lo, tot_hi, tot_lo)], 1
        )
        n_stat = kv_local * group_size
        pad = (-stats.shape[1]) % 128
        stats = jnp.pad(stats, ((0, 0), (0, pad)))
        packed = to_bf16(jnp.concatenate([req_weighted.reshape(req_count, -1), stats], 1))
        packed = packed.reshape(n_mem, rows, -1)
        pieces = [lax.dynamic_index_in_dim(packed, mem_pos, 0, False)]
        pieces += scatter_parts(packed, "mem", n_mem)
        peaks, totals, tops = [], [], []
        for piece in pieces:
            st = piece[:, q_width : q_width + 4 * n_stat].astype(jnp.float32)
            st = st.reshape(rows, 4, kv_local, group_size)
            peaks.append(st[:, 0] + st[:, 1])
            totals.append(st[:, 2] + st[:, 3])
            tops.append(
                piece[:, :q_width]
                .astype(jnp.float32)
                .reshape(rows, kv_local, group_size, head_dim)
            )
        peak = own_score
        for p in peaks:
            peak = jnp.maximum(peak, p)
        own_weight = jnp.exp(own_score - peak)
        denom = own_weight
        numer = own_weight[..., None] * new_values.astype(jnp.float32)[:, :, None, :]
        for p, t, w in zip(peaks, totals, tops):
            f = jnp.exp(p - peak)
            denom = denom + t * f
            numer = numer + w * f[..., None]
        attended_own = to_bf16(numer / denom[..., None]).reshape(rows, -1)
        if rows % 8:
            attended = gather_parts(attended_own, "mem", n_mem)

            comp_pos = lax.axis_index("comp")
            rows_c = req_count // n_comp
            attn_proj = jnp.dot(attended, w_out, preferred_element_type=jnp.float32)
            resid_own = lax.dynamic_slice_in_dim(hidden_in, comp_pos * rows_c, rows_c, 0)
            middle_own = to_bf16(resid_own.astype(jnp.float32) + summed(attn_proj, "comp", n_comp))
            middle = gather_parts(middle_own, "comp", n_comp)
            middle_wide = middle.astype(jnp.float32)
            normed_ffn = to_bf16(middle_wide * ffn_gain.astype(jnp.float32))
            gate_up = jnp.einsum(
                "rd,dtf->rtf", normed_ffn, w_gate_up, preferred_element_type=jnp.float32
            ).reshape(req_count, -1)
            m_hi, m_lo = split_hi_lo(jnp.sum(middle_wide * middle_wide, 1))
            wide = jnp.concatenate(
                [
                    to_bf16(gate_up),
                    jnp.broadcast_to(m_hi[:, None], (req_count, 128)),
                    jnp.broadcast_to(m_lo[:, None], (req_count, 128)),
                ],
                1,
            ).reshape(n_mem, rows, -1)
            total = lax.dynamic_index_in_dim(wide, mem_pos, 0, False).astype(jnp.float32)
            for part in scatter_parts(wide, "mem", n_mem):
                total = total + part.astype(jnp.float32)
            ff = w_gate_up.shape[2]
            ffn_scale = lax.rsqrt((total[:, 2 * ff] + total[:, 2 * ff + 128]) / D + NORM_EPS)
            gate = total[:, :ff] * ffn_scale[:, None]
            up = total[:, ff : 2 * ff] * ffn_scale[:, None]
            activated = gather_parts(to_bf16(jax.nn.silu(gate) * up), "mem", n_mem)
            down_part = jnp.dot(activated, w_down, preferred_element_type=jnp.float32)
            updated_own = to_bf16(middle_own.astype(jnp.float32) + summed(down_part, "comp", n_comp))
            updated = gather_parts(updated_own, "comp", n_comp)
            return (attended, updated)

        depth = w_gate_up.shape[0]
        cut_a, cut_b = depth * CUT[0] // 16, depth * CUT[1] // 16
        gate_a = fetch(w_gate_up, 0, cut_a, attended_own)
        proj, attended = gathered_dot(
            around(attended_own, "mem", n_mem), out_held, n_mem, True, (gate_a,)
        )
        near, far = pairwise(proj, n_comp, 0.0)
        gate_b = fetch(w_gate_up, cut_a, cut_b, near)
        middle, *terms = gate_up_parts(
            hidden_in, near, far, ffn_gain, (gate_a, gate_b), w_gate_up, n_mem, 0.0
        )
        down_held = fetch(w_down, 0, w_down.shape[0], terms[0])
        terms = terms[:1] + [shifted(t, "mem", n_mem, s) for s, t in enumerate(terms) if s]
        activated = activate(terms, (down_held,))
        (down,) = gathered_dot(
            around(activated, "mem", n_mem), down_held, n_mem, False
        )
        near, far = pairwise(down, n_comp, 0.0)
        updated = to_bf16(
            middle.astype(jnp.float32) + (near.astype(jnp.float32) + far.astype(jnp.float32))
        )
        return (attended, updated)

    return shards


def solution(mesh):
    in_specs = (
        P("groups", "mem"),
        P("groups"),
        P("groups", None),
        P(("groups", "mem"), None, "comp"),
        P(("groups", "mem"), None, "comp"),
        P("mem"),
        P("mem", "comp"),
        P("mem", None, "comp"),
        P("comp", "mem"),
        P("mem"),
        P("mem", None, "comp"),
        P("comp", "mem"),
    )
    out_specs = (P("groups", "comp"), P("groups", "mem"))
    return jax.shard_map(
        make_shards(mesh.shape["mem"], mesh.shape["comp"]),
        mesh=mesh,
        in_specs=in_specs,
        out_specs=out_specs,
        check_vma=False,
    )
```

```python
import math

import jax
import jax.numpy as jnp
from jax import lax
from jax.experimental import pallas as pl
from jax.experimental.pallas import tpu as pltpu
from jax.sharding import PartitionSpec as P

D = 8192
HD = 128
NORM_EPS = 1e-05
ROPE_BASE = 500000.0
NEG_FILL = -1e30


def to_bf16(x):
    return x.astype(jnp.bfloat16)


def shifted(x, axis, n, step):
    return lax.ppermute(x, axis, [(i, (i + step) % n) for i in range(n)])


def split_hi_lo(x):
    hi = lax.reduce_precision(x, 8, 7)
    return to_bf16(hi), to_bf16(x - hi)


def scatter_parts(x, axis, n):
    me = lax.axis_index(axis)
    parts = []
    for step in range(1, n):
        send = lax.dynamic_index_in_dim(x, (me + step) % n, 0, False)
        parts.append(shifted(send, axis, n, step))
    return parts


def gather_parts(x, axis, n):
    me = lax.axis_index(axis)
    parts = [shifted(x, axis, n, step) for step in range(n - 1, 0, -1)] + [x]
    both = jnp.concatenate(parts + parts, 0)
    rows = x.shape[0]
    return lax.dynamic_slice_in_dim(both, (n - 1 - me) * rows, n * rows, 0)


def summed(x, axis, n):
    me = lax.axis_index(axis)
    rows = x.shape[0] // n
    x = x.reshape((n, rows) + x.shape[1:])
    own = lax.dynamic_index_in_dim(x, me, 0, False)
    for part in scatter_parts(to_bf16(x), axis, n):
        own = own + part.astype(jnp.float32)
    return own


VMEM = pltpu.VMEM
LIMIT = 12 << 20
GATE_LIMIT = 24 << 20
QUERY_LIMIT = 56 << 20
FETCH_LIMIT = 26 << 20
CUT = (6, 5)
OUT_LIMIT = 40 << 20


def whole(count):
    return [pl.BlockSpec(memory_space=VMEM)] * count


def cost(hidden_us=0.0, weight=None, rows=32):
    size = 0 if weight is None else weight.size
    return pl.CostEstimate(
        flops=2 * rows * size,
        bytes_accessed=int(2 * size + hidden_us * 3e6),
        transcendentals=0,
    )


def place(parts, held, n_mem):
    me = lax.axis_index("mem")
    rows = parts[0].shape[0]
    for step, part in enumerate(parts):
        at = pl.multiple_of(lax.rem(me - step + n_mem, n_mem) * rows, rows)
        held[pl.ds(at, rows), :] = part[...].astype(jnp.float32)


def fetch(weight, start, count, after, limit=None):
    pieces = 4
    step = count // pieces

    def kernel(after_ref, w_ref, out, sems):
        copies = [
            pltpu.make_async_copy(
                w_ref.at[pl.ds(start + i * step, step)], out.at[pl.ds(i * step, step)], sems.at[i]
            )
            for i in range(pieces)
        ]
        for copy in copies:
            copy.start()
        for copy in copies:
            copy.wait()

    return pl.pallas_call(
        kernel,
        in_specs=[pl.BlockSpec(memory_space=pl.ANY)] * 2,
        out_specs=pl.BlockSpec(memory_space=VMEM),
        out_shape=jax.ShapeDtypeStruct((count,) + weight.shape[1:], weight.dtype),
        scratch_shapes=[pltpu.SemaphoreType.DMA((pieces,))],
        compiler_params=pltpu.CompilerParams(vmem_limit_bytes=FETCH_LIMIT if limit is None else limit),
        cost_estimate=pl.CostEstimate(
            flops=700 * count * math.prod(weight.shape[1:]),
            bytes_accessed=0,
            transcendentals=0,
        ),
    )(after, weight)


def tiled_dot(x, w_ref, out_ref, tile):
    @pl.loop(0, w_ref.shape[-1] // tile)
    def _(i):
        cols = pl.ds(pl.multiple_of(i * tile, tile), tile)
        out_ref[:, cols] = jnp.dot(
            x, w_ref[:, cols], preferred_element_type=jnp.float32
        ).astype(out_ref.dtype)


def gathered_dot(parts, weight, n_mem, keep, beside=()):
    rows = parts[0].shape[0] * n_mem
    depth, width = weight.shape
    tile = width

    def kernel(*refs):
        part_refs, w_ref = refs[:n_mem], refs[n_mem]
        outs, held = refs[n_mem + 1 + len(beside) : -1], refs[-1]
        place(part_refs, held, n_mem)
        x = to_bf16(held[...])
        if keep:
            outs[1][...] = x
        tiled_dot(x, w_ref, outs[0], tile)

    shapes = [jax.ShapeDtypeStruct((rows, width), jnp.bfloat16)]
    if keep:
        shapes.append(jax.ShapeDtypeStruct((rows, depth), jnp.bfloat16))
    return pl.pallas_call(
        kernel,
        in_specs=whole(n_mem + 1) + [pl.BlockSpec(memory_space=pl.ANY)] * len(beside),
        out_specs=whole(len(shapes)),
        out_shape=shapes,
        scratch_shapes=[VMEM((rows, depth), jnp.float32)],
        compiler_params=pltpu.CompilerParams(vmem_limit_bytes=LIMIT),
        cost_estimate=cost(0.0, weight),
    )(*parts, weight, *beside)


def unfold(x, spread):
    count = x.shape[0]
    row = lax.broadcasted_iota(jnp.int32, (128, 256), 0)
    col = lax.broadcasted_iota(jnp.int32, (128, 256), 1)
    even = jnp.where(col == 2 * row, 1.0, 0.0).astype(jnp.bfloat16)
    odd = jnp.where(col == 2 * row + 1, 1.0, 0.0).astype(jnp.bfloat16)
    for b in range(x.shape[1] // 128):
        block = x[:, b * 128 : (b + 1) * 128]
        for half, pick in enumerate((even, odd)):
            spread[half * count : (half + 1) * count, b * 256 : (b + 1) * 256] = to_bf16(
                jnp.dot(block, pick, preferred_element_type=jnp.float32)
            )


def query_parts(hidden, gain, w_query, w_kv, n_mem):
    req, depth = hidden.shape
    q_width, kv_width = w_query.shape[1], w_kv.shape[2]
    rows = req // n_mem
    body = q_width + 2 * kv_width
    chunks, ahead = 8, 5
    step = depth // chunks

    def kernel(hid_ref, gain_ref, wq_ref, wkv_ref, *refs):
        outs = refs[:n_mem]
        acc, spread, q_buf, kv_buf, q_sems, kv_sems, hid_buf, gain_buf = refs[n_mem:]
        small = [
            pltpu.make_async_copy(hid_ref, hid_buf, kv_sems.at[1]),
            pltpu.make_async_copy(gain_ref, gain_buf, kv_sems.at[2]),
        ]
        for copy in small:
            copy.start()
        kv_copy = pltpu.make_async_copy(wkv_ref, kv_buf, kv_sems.at[0])
        kv_copy.start()
        copies = [
            pltpu.make_async_copy(
                wq_ref.at[pl.ds(i * step, step)], q_buf.at[pl.ds(i * step, step)], q_sems.at[i]
            )
            for i in range(chunks)
        ]
        for copy in copies[:ahead]:
            copy.start()
        for copy in small:
            copy.wait()
        wide = hid_buf[...].astype(jnp.float32)
        acc[:, body:] = jnp.broadcast_to(jnp.sum(wide * wide, 1, keepdims=True), (req, 128))
        normed = to_bf16(wide * gain_buf[...].astype(jnp.float32).reshape(1, depth))
        unfold(normed, spread)
        for i, copy in enumerate(copies):
            copy.wait()
            if i + ahead < chunks:
                copies[i + ahead].start()
            term = jnp.dot(
                normed[:, i * step : (i + 1) * step],
                q_buf[i * step : (i + 1) * step, :],
                preferred_element_type=jnp.float32,
            )
            acc[:, :q_width] = term if i == 0 else acc[:, :q_width] + term
        kv_copy.wait()
        both = jnp.dot(
            spread[...],
            kv_buf[...].reshape(2 * depth, kv_width),
            preferred_element_type=jnp.float32,
        )
        acc[:, q_width : q_width + kv_width] = both[:req]
        acc[:, q_width + kv_width : body] = both[req:]
        me = lax.axis_index("mem")
        for step_to in range(n_mem):
            at = pl.multiple_of(lax.rem(me + step_to, n_mem) * rows, rows)
            outs[step_to][...] = acc[pl.ds(at, rows), :]

    return pl.pallas_call(
        kernel,
        in_specs=[pl.BlockSpec(memory_space=pltpu.HBM)] * 4,
        out_specs=whole(n_mem),
        out_shape=[jax.ShapeDtypeStruct((rows, body + 128), jnp.float32)] * n_mem,
        scratch_shapes=[
            VMEM((req, body + 128), jnp.float32),
            VMEM((2 * req, 2 * depth), jnp.bfloat16),
            VMEM(w_query.shape, jnp.bfloat16),
            VMEM(w_kv.shape, jnp.bfloat16),
            pltpu.SemaphoreType.DMA((chunks,)),
            pltpu.SemaphoreType.DMA((3,)),
            VMEM(hidden.shape, jnp.bfloat16),
            VMEM(gain.shape, jnp.bfloat16),
        ],
        compiler_params=pltpu.CompilerParams(vmem_limit_bytes=QUERY_LIMIT),
        cost_estimate=pl.CostEstimate(
            flops=2 * req * w_query.size, bytes_accessed=2 * w_query.size, transcendentals=0
        ),
    )(hidden, gain, w_query, w_kv)


def turned_parts(parts, cosine, sine, q_width, kv_width, beside):
    rows = parts[0].shape[0]
    body = q_width + 2 * kv_width
    n = len(parts)

    def kernel(*refs):
        cos_ref, sin_ref, out = refs[n], refs[n + 1], refs[-1]
        total = refs[0][...]
        for ref in refs[1:n]:
            total = total + ref[...]
        scale = lax.rsqrt(total[:, body : body + 1] / D + NORM_EPS)
        cos, sin = cos_ref[...], sin_ref[...]
        for at in range(0, q_width + kv_width, HD):
            head = total[:, at : at + HD] * scale
            out[:, at : at + HD] = to_bf16(head * cos + pltpu.roll(head, HD // 2, 1) * sin)
        out[:, q_width + kv_width :] = to_bf16(total[:, q_width + kv_width : body] * scale)

    return pl.pallas_call(
        kernel,
        in_specs=whole(n + 2) + [pl.BlockSpec(memory_space=pl.ANY)] * len(beside),
        out_specs=pl.BlockSpec(memory_space=VMEM),
        out_shape=jax.ShapeDtypeStruct((rows, body), jnp.bfloat16),
        compiler_params=pltpu.CompilerParams(vmem_limit_bytes=LIMIT),
        cost_estimate=cost(0.0),
    )(*parts, cosine, sine, *beside)


def gate_up_parts(hidden, near, far, gain, held, weight, n_mem, hidden_us):
    req, depth = hidden.shape
    ff = weight.shape[2]
    rows = req // n_mem
    tile = ff // 2 if ff % 256 == 0 else 128

    n_held = len(held)
    first = sum(h.shape[0] for h in held)
    rest = depth - first
    chunk = 128

    def kernel(hid_ref, near_ref, far_ref, gain_ref, *refs):
        held_refs, w_ref, mid_ref = refs[:n_held], refs[n_held], refs[n_held + 1]
        outs, (spread, acc, power, tail, sems) = (
            refs[n_held + 2 : n_held + 2 + n_mem],
            refs[n_held + 2 + n_mem :],
        )
        copies = [
            pltpu.make_async_copy(
                w_ref.at[pl.ds(first + i * chunk, chunk)],
                tail.at[pl.ds(i * chunk, chunk)],
                sems.at[i],
            )
            for i in range(rest // chunk)
        ]
        for copy in copies:
            copy.start()
        total = near_ref[...].astype(jnp.float32) + far_ref[...].astype(jnp.float32)
        middle = to_bf16(hid_ref[...].astype(jnp.float32) + total)
        mid_ref[...] = middle
        wide = middle.astype(jnp.float32)
        power[...] = jnp.broadcast_to(jnp.sum(wide * wide, 1, keepdims=True), power.shape)
        normed = to_bf16(wide * gain_ref[...].astype(jnp.float32).reshape(1, depth))
        unfold(normed, spread)

        def add_rows(block, at, count, fresh):
            @pl.loop(0, ff // tile)
            def _(i):
                cols = pl.ds(pl.multiple_of(i * tile, tile), tile)
                term = jnp.dot(
                    spread[:, 2 * at : 2 * (at + count)],
                    block[:, :, cols].reshape(2 * count, tile),
                    preferred_element_type=jnp.float32,
                )
                acc[:, cols] = term if fresh else acc[:, cols] + term

        at = 0
        for ref in held_refs:
            add_rows(ref, at, ref.shape[0], at == 0)
            at += ref.shape[0]
        for copy in copies:
            copy.wait()
        if rest:
            add_rows(tail, first, rest, first == 0)

        me = lax.axis_index("mem")
        for step in range(n_mem):
            at = pl.multiple_of(lax.rem(me + step, n_mem) * rows, rows)
            out = outs[step]
            gate = acc[pl.ds(at, rows), :]
            up = acc[pl.ds(at + req, rows), :]
            out[:, :ff] = to_bf16(jnp.concatenate([gate, up], 0))
            pw = power[pl.ds(at, rows), :]
            hi = to_bf16(pw).astype(jnp.float32)
            out[:, ff:] = to_bf16(jnp.concatenate([hi, pw - hi], 0))

    return pl.pallas_call(
        kernel,
        in_specs=whole(4 + n_held) + [pl.BlockSpec(memory_space=pl.ANY)],
        out_specs=whole(n_mem + 1),
        out_shape=[jax.ShapeDtypeStruct((req, depth), jnp.bfloat16)]
        + [jax.ShapeDtypeStruct((2 * rows, ff + 128), jnp.bfloat16)] * n_mem,
        scratch_shapes=[
            VMEM((2 * req, 2 * depth), jnp.bfloat16),
            VMEM((2 * req, ff), jnp.float32),
            VMEM((req, 128), jnp.float32),
            VMEM((max(rest, chunk), 2, ff), jnp.bfloat16),
            pltpu.SemaphoreType.DMA((max(rest // chunk, 1),)),
        ],
        compiler_params=pltpu.CompilerParams(vmem_limit_bytes=GATE_LIMIT),
        cost_estimate=cost(hidden_us, weight, 64),
    )(hidden, near, far, gain, *held, weight)


def activate(parts, beside):
    rows = parts[0].shape[0] // 2
    ff = parts[0].shape[1] - 128

    def kernel(*refs):
        out = refs[-1]
        total = refs[0][...].astype(jnp.float32)
        for ref in refs[1 : len(parts)]:
            total = total + ref[...].astype(jnp.float32)
        power = total[:rows, ff : ff + 1] + total[rows:, ff : ff + 1]
        scale = lax.rsqrt(power / D + NORM_EPS)
        gate = total[:rows, :ff] * scale
        up = total[rows:, :ff] * scale
        out[...] = to_bf16(gate / (1.0 + jnp.exp(-gate)) * up)

    return pl.pallas_call(
        kernel,
        in_specs=whole(len(parts)) + [pl.BlockSpec(memory_space=pl.ANY)] * len(beside),
        out_specs=pl.BlockSpec(memory_space=VMEM),
        out_shape=jax.ShapeDtypeStruct((rows, ff), jnp.bfloat16),
        compiler_params=pltpu.CompilerParams(vmem_limit_bytes=LIMIT),
        cost_estimate=cost(0.0),
    )(*parts, *beside)


def around(x, axis, n):
    return [x] + [shifted(x, axis, n, step) for step in range(1, n)]


def added(left, right, hidden_us):
    def kernel(l_ref, r_ref, out):
        out[...] = to_bf16(l_ref[...].astype(jnp.float32) + r_ref[...].astype(jnp.float32))

    return pl.pallas_call(
        kernel,
        in_specs=whole(2),
        out_specs=pl.BlockSpec(memory_space=VMEM),
        out_shape=jax.ShapeDtypeStruct(left.shape, left.dtype),
        compiler_params=pltpu.CompilerParams(vmem_limit_bytes=LIMIT),
        cost_estimate=cost(hidden_us),
    )(left, right)


def pairwise(x, n, hidden_us):
    near, step = x, 1
    while True:
        far = lax.ppermute(near, "comp", [(i, i ^ step) for i in range(n)])
        step *= 2
        if step >= n:
            return near, far
        near = added(near, far, hidden_us)


def rotary(positions, head_dim):
    half_dim = head_dim // 2
    freq_steps = jnp.arange(half_dim, dtype=jnp.float32) * (2.0 / head_dim)
    inv_freq = jnp.exp(-freq_steps * math.log(ROPE_BASE))
    angles = positions.astype(jnp.float32)[:, None, None] * inv_freq
    return jnp.cos(angles), jnp.sin(angles)


def rotate(values, cosine, sine):
    half_dim = values.shape[-1] // 2
    first_half = values[..., :half_dim]
    second_half = values[..., half_dim:]
    return jnp.concatenate(
        [first_half * cosine - second_half * sine, second_half * cosine + first_half * sine], -1
    )


def slot_stats(queries_slot, key_rows, value_rows, slot_fill, scale_val):
    scores = (
        jnp.einsum("skgd,sbkd->skgb", queries_slot, key_rows, preferred_element_type=jnp.float32)
        * scale_val
    )
    is_valid = (jnp.arange(key_rows.shape[1], dtype=jnp.int32)[None, :] < slot_fill[:, None])[
        :, None, None, :
    ]
    scores = jnp.where(is_valid, scores, NEG_FILL)
    peak_val = jnp.max(scores, -1)
    weights = jnp.where(is_valid, jnp.exp(scores - peak_val[..., None]), 0.0)
    total_w = jnp.sum(weights, -1)
    weighted = jnp.einsum(
        "skgb,sbkd->skgd",
        weights.astype(jnp.bfloat16),
        value_rows,
        preferred_element_type=jnp.float32,
    )
    return (peak_val, total_w, weighted)


def make_shards(n_mem, n_comp):
    def shards(
        hidden_in,
        lengths,
        block_table,
        cache_keys,
        cache_values,
        attn_gain,
        w_query,
        w_kv,
        w_out,
        ffn_gain,
        w_gate_up,
        w_down,
    ):
        highest = lax.Precision.HIGHEST
        req_count = hidden_in.shape[0]
        slot_count, blk_len, kv_width = cache_keys.shape
        head_dim = HD
        kv_local = kv_width // head_dim
        q_width = w_query.shape[1]
        group_size = q_width // kv_width
        scale_val = 1.0 / math.sqrt(head_dim)
        mem_pos = lax.axis_index("mem")
        rows = req_count // n_mem
        if rows % 8:
            resid = hidden_in.astype(jnp.float32)
            normed = to_bf16(resid * attn_gain.astype(jnp.float32))
            query_part = jnp.dot(normed, w_query, preferred_element_type=jnp.float32)
            kv_part = jnp.dot(
                normed, w_kv.reshape(w_kv.shape[0], -1), preferred_element_type=jnp.float32
            )
            power = jnp.sum(resid * resid, 1)
            wide = jnp.concatenate(
                [query_part, kv_part, jnp.broadcast_to(power[:, None], (req_count, 128))], 1
            ).reshape(n_mem, rows, -1)
            total = lax.dynamic_index_in_dim(wide, mem_pos, 0, False)
            for part in scatter_parts(wide, "mem", n_mem):
                total = total + part
            body = q_width + 2 * kv_width
            attn_scale = lax.rsqrt(total[:, body] / D + NORM_EPS)
            cosine, sine = rotary(lengths, head_dim)
            cos_own = lax.dynamic_slice_in_dim(cosine, mem_pos * rows, rows, 0)
            sin_own = lax.dynamic_slice_in_dim(sine, mem_pos * rows, rows, 0)
            scaled = total[:, :body] * attn_scale[:, None]
            turned = rotate(
                scaled[:, : q_width + kv_width].reshape(rows, -1, head_dim), cos_own, sin_own
            ).reshape(rows, -1)
            own_qkv = to_bf16(jnp.concatenate([turned, scaled[:, q_width + kv_width :]], 1))
        else:
            here = lax.dynamic_slice_in_dim(lengths, mem_pos * rows, rows, 0)
            cosine, sine = rotary(here, head_dim)
            cosine = jnp.concatenate([cosine, cosine], -1)[:, 0]
            sine = jnp.concatenate([-sine, sine], -1)[:, 0]
            terms = list(query_parts(hidden_in, attn_gain, w_query, w_kv, n_mem))
            out_held = fetch(w_out, 0, w_out.shape[0], terms[0], OUT_LIMIT)
            terms = terms[:1] + [shifted(t, "mem", n_mem, s) for s, t in enumerate(terms) if s]
            own_qkv = turned_parts(terms, cosine, sine, q_width, kv_width, (out_held,))
        qkv = gather_parts(own_qkv, "mem", n_mem)
        queries = qkv[:, :q_width].reshape(req_count, kv_local, group_size, head_dim)
        q_own = own_qkv[:, :q_width].reshape(rows, kv_local, group_size, head_dim)
        new_keys = own_qkv[:, q_width : q_width + kv_width].reshape(rows, kv_local, head_dim)
        new_values = own_qkv[:, q_width + kv_width :].reshape(rows, kv_local, head_dim)
        own_score = (
            jnp.einsum("rkgd,rkd->rkg", q_own, new_keys, preferred_element_type=jnp.float32)
            * scale_val
        )

        blk_count = block_table.shape[1]
        block_first = jnp.arange(blk_count, dtype=jnp.int32) * blk_len
        is_live = block_first[None, :] < lengths[:, None]
        local_slot = block_table - mem_pos * slot_count
        slot_ids = jnp.arange(slot_count, dtype=jnp.int32)
        owners = is_live[:, :, None] & (local_slot[:, :, None] == slot_ids[None, None, :])
        slot_member = jnp.any(owners, 1).T
        block_fill = jnp.clip(lengths[:, None] - block_first[None, :], 0, blk_len)
        slot_fill = jnp.sum(jnp.where(owners, block_fill[:, :, None], 0), (0, 1))
        queries_slot = jnp.dot(
            slot_member.astype(jnp.bfloat16),
            queries.reshape(req_count, -1),
            preferred_element_type=jnp.float32,
        )
        queries_slot = queries_slot.astype(jnp.bfloat16).reshape(
            slot_count, kv_local, group_size, head_dim
        )
        key_rows = cache_keys.reshape(slot_count, blk_len, kv_local, head_dim)
        value_rows = cache_values.reshape(slot_count, blk_len, kv_local, head_dim)
        peak_val, total_w, weighted = slot_stats(
            queries_slot, key_rows, value_rows, slot_fill, scale_val
        )
        member_mask = slot_member[:, :, None, None]
        req_peak = jnp.max(jnp.where(member_mask, peak_val[:, None], NEG_FILL), 0)
        peak_hi = lax.reduce_precision(req_peak, 8, 7)
        peak_lo = lax.reduce_precision(req_peak - peak_hi, 8, 7)
        req_peak = peak_hi + peak_lo
        slot_ref = jnp.min(jnp.where(member_mask, req_peak[None], -NEG_FILL), 1)
        factor = jnp.exp(peak_val - slot_ref)
        member_wide = slot_member.astype(jnp.float32)
        req_total = jnp.einsum("sr,skg->rkg", member_wide, total_w * factor, precision=highest)
        req_weighted = jnp.einsum(
            "sr,skgd->rkgd", member_wide, weighted * factor[..., None], precision=highest
        )
        tot_hi = lax.reduce_precision(req_total, 8, 7)
        tot_lo = req_total - tot_hi
        stats = jnp.concatenate(
            [s.reshape(req_count, -1) for s in (peak_hi, peak_lo, tot_hi, tot_lo)], 1
        )
        n_stat = kv_local * group_size
        pad = (-stats.shape[1]) % 128
        stats = jnp.pad(stats, ((0, 0), (0, pad)))
        packed = to_bf16(jnp.concatenate([req_weighted.reshape(req_count, -1), stats], 1))
        packed = packed.reshape(n_mem, rows, -1)
        pieces = [lax.dynamic_index_in_dim(packed, mem_pos, 0, False)]
        pieces += scatter_parts(packed, "mem", n_mem)
        peaks, totals, tops = [], [], []
        for piece in pieces:
            st = piece[:, q_width : q_width + 4 * n_stat].astype(jnp.float32)
            st = st.reshape(rows, 4, kv_local, group_size)
            peaks.append(st[:, 0] + st[:, 1])
            totals.append(st[:, 2] + st[:, 3])
            tops.append(
                piece[:, :q_width]
                .astype(jnp.float32)
                .reshape(rows, kv_local, group_size, head_dim)
            )
        peak = own_score
        for p in peaks:
            peak = jnp.maximum(peak, p)
        own_weight = jnp.exp(own_score - peak)
        denom = own_weight
        numer = own_weight[..., None] * new_values.astype(jnp.float32)[:, :, None, :]
        for p, t, w in zip(peaks, totals, tops):
            f = jnp.exp(p - peak)
            denom = denom + t * f
            numer = numer + w * f[..., None]
        attended_own = to_bf16(numer / denom[..., None]).reshape(rows, -1)
        if rows % 8:
            attended = gather_parts(attended_own, "mem", n_mem)

            comp_pos = lax.axis_index("comp")
            rows_c = req_count // n_comp
            attn_proj = jnp.dot(attended, w_out, preferred_element_type=jnp.float32)
            resid_own = lax.dynamic_slice_in_dim(hidden_in, comp_pos * rows_c, rows_c, 0)
            middle_own = to_bf16(resid_own.astype(jnp.float32) + summed(attn_proj, "comp", n_comp))
            middle = gather_parts(middle_own, "comp", n_comp)
            middle_wide = middle.astype(jnp.float32)
            normed_ffn = to_bf16(middle_wide * ffn_gain.astype(jnp.float32))
            gate_up = jnp.einsum(
                "rd,dtf->rtf", normed_ffn, w_gate_up, preferred_element_type=jnp.float32
            ).reshape(req_count, -1)
            m_hi, m_lo = split_hi_lo(jnp.sum(middle_wide * middle_wide, 1))
            wide = jnp.concatenate(
                [
                    to_bf16(gate_up),
                    jnp.broadcast_to(m_hi[:, None], (req_count, 128)),
                    jnp.broadcast_to(m_lo[:, None], (req_count, 128)),
                ],
                1,
            ).reshape(n_mem, rows, -1)
            total = lax.dynamic_index_in_dim(wide, mem_pos, 0, False).astype(jnp.float32)
            for part in scatter_parts(wide, "mem", n_mem):
                total = total + part.astype(jnp.float32)
            ff = w_gate_up.shape[2]
            ffn_scale = lax.rsqrt((total[:, 2 * ff] + total[:, 2 * ff + 128]) / D + NORM_EPS)
            gate = total[:, :ff] * ffn_scale[:, None]
            up = total[:, ff : 2 * ff] * ffn_scale[:, None]
            activated = gather_parts(to_bf16(jax.nn.silu(gate) * up), "mem", n_mem)
            down_part = jnp.dot(activated, w_down, preferred_element_type=jnp.float32)
            updated_own = to_bf16(middle_own.astype(jnp.float32) + summed(down_part, "comp", n_comp))
            updated = gather_parts(updated_own, "comp", n_comp)
            return (attended, updated)

        depth = w_gate_up.shape[0]
        cut_a, cut_b = depth * CUT[0] // 16, depth * CUT[1] // 16
        gate_a = fetch(w_gate_up, 0, cut_a, attended_own)
        proj, attended = gathered_dot(
            around(attended_own, "mem", n_mem), out_held, n_mem, True, (gate_a,)
        )
        near, far = pairwise(proj, n_comp, 0.0)
        gate_b = fetch(w_gate_up, cut_a, cut_b, near)
        middle, *terms = gate_up_parts(
            hidden_in, near, far, ffn_gain, (gate_a, gate_b), w_gate_up, n_mem, 0.0
        )
        down_held = fetch(w_down, 0, w_down.shape[0], terms[0])
        terms = terms[:1] + [shifted(t, "mem", n_mem, s) for s, t in enumerate(terms) if s]
        activated = activate(terms, (down_held,))
        (down,) = gathered_dot(
            around(activated, "mem", n_mem), down_held, n_mem, False
        )
        near, far = pairwise(down, n_comp, 0.0)
        updated = to_bf16(
            middle.astype(jnp.float32) + (near.astype(jnp.float32) + far.astype(jnp.float32))
        )
        return (attended, updated)

    return shards


def solution(mesh):
    in_specs = (
        P("groups", "mem"),
        P("groups"),
        P("groups", None),
        P(("groups", "mem"), None, "comp"),
        P(("groups", "mem"), None, "comp"),
        P("mem"),
        P("mem", "comp"),
        P("mem", None, "comp"),
        P("comp", "mem"),
        P("mem"),
        P("mem", None, "comp"),
        P("comp", "mem"),
    )
    out_specs = (P("groups", "comp"), P("groups", "mem"))
    return jax.shard_map(
        make_shards(mesh.shape["mem"], mesh.shape["comp"]),
        mesh=mesh,
        in_specs=in_specs,
        out_specs=out_specs,
        check_vma=False,
    )
```

```python
import math

import jax
import jax.numpy as jnp
from jax import lax
from jax.experimental import pallas as pl
from jax.experimental.pallas import tpu as pltpu
from jax.sharding import PartitionSpec as P

D = 8192
HD = 128
NORM_EPS = 1e-05
ROPE_BASE = 500000.0
NEG_FILL = -1e30


def to_bf16(x):
    return x.astype(jnp.bfloat16)


def shifted(x, axis, n, step):
    return lax.ppermute(x, axis, [(i, (i + step) % n) for i in range(n)])


def split_hi_lo(x):
    hi = lax.reduce_precision(x, 8, 7)
    return to_bf16(hi), to_bf16(x - hi)


def scatter_parts(x, axis, n):
    me = lax.axis_index(axis)
    parts = []
    for step in range(1, n):
        send = lax.dynamic_index_in_dim(x, (me + step) % n, 0, False)
        parts.append(shifted(send, axis, n, step))
    return parts


def gather_parts(x, axis, n):
    me = lax.axis_index(axis)
    parts = [shifted(x, axis, n, step) for step in range(n - 1, 0, -1)] + [x]
    both = jnp.concatenate(parts + parts, 0)
    rows = x.shape[0]
    return lax.dynamic_slice_in_dim(both, (n - 1 - me) * rows, n * rows, 0)


def summed(x, axis, n):
    me = lax.axis_index(axis)
    rows = x.shape[0] // n
    x = x.reshape((n, rows) + x.shape[1:])
    own = lax.dynamic_index_in_dim(x, me, 0, False)
    for part in scatter_parts(to_bf16(x), axis, n):
        own = own + part.astype(jnp.float32)
    return own


VMEM = pltpu.VMEM
LIMIT = 12 << 20
GATE_LIMIT = 24 << 20
QUERY_LIMIT = 56 << 20
FETCH_LIMIT = 26 << 20
CUT = (7, 5)
OUT_LIMIT = 40 << 20


def whole(count):
    return [pl.BlockSpec(memory_space=VMEM)] * count


def cost(hidden_us=0.0, weight=None, rows=32):
    size = 0 if weight is None else weight.size
    return pl.CostEstimate(
        flops=2 * rows * size,
        bytes_accessed=int(2 * size + hidden_us * 3e6),
        transcendentals=0,
    )


def place(parts, held, n_mem):
    me = lax.axis_index("mem")
    rows = parts[0].shape[0]
    for step, part in enumerate(parts):
        at = pl.multiple_of(lax.rem(me - step + n_mem, n_mem) * rows, rows)
        held[pl.ds(at, rows), :] = part[...].astype(jnp.float32)


def fetch(weight, start, count, after, limit=None):
    pieces = 4
    step = count // pieces

    def kernel(after_ref, w_ref, out, sems):
        copies = [
            pltpu.make_async_copy(
                w_ref.at[pl.ds(start + i * step, step)], out.at[pl.ds(i * step, step)], sems.at[i]
            )
            for i in range(pieces)
        ]
        for copy in copies:
            copy.start()
        for copy in copies:
            copy.wait()

    return pl.pallas_call(
        kernel,
        in_specs=[pl.BlockSpec(memory_space=pl.ANY)] * 2,
        out_specs=pl.BlockSpec(memory_space=VMEM),
        out_shape=jax.ShapeDtypeStruct((count,) + weight.shape[1:], weight.dtype),
        scratch_shapes=[pltpu.SemaphoreType.DMA((pieces,))],
        compiler_params=pltpu.CompilerParams(vmem_limit_bytes=FETCH_LIMIT if limit is None else limit),
        cost_estimate=pl.CostEstimate(
            flops=700 * count * math.prod(weight.shape[1:]),
            bytes_accessed=0,
            transcendentals=0,
        ),
    )(after, weight)


def tiled_dot(x, w_ref, out_ref, tile):
    @pl.loop(0, w_ref.shape[-1] // tile)
    def _(i):
        cols = pl.ds(pl.multiple_of(i * tile, tile), tile)
        out_ref[:, cols] = jnp.dot(
            x, w_ref[:, cols], preferred_element_type=jnp.float32
        ).astype(out_ref.dtype)


def gathered_dot(parts, weight, n_mem, keep, beside=()):
    rows = parts[0].shape[0] * n_mem
    depth, width = weight.shape
    tile = width

    def kernel(*refs):
        part_refs, w_ref = refs[:n_mem], refs[n_mem]
        outs, held = refs[n_mem + 1 + len(beside) : -1], refs[-1]
        place(part_refs, held, n_mem)
        x = to_bf16(held[...])
        if keep:
            outs[1][...] = x
        tiled_dot(x, w_ref, outs[0], tile)

    shapes = [jax.ShapeDtypeStruct((rows, width), jnp.bfloat16)]
    if keep:
        shapes.append(jax.ShapeDtypeStruct((rows, depth), jnp.bfloat16))
    return pl.pallas_call(
        kernel,
        in_specs=whole(n_mem + 1) + [pl.BlockSpec(memory_space=pl.ANY)] * len(beside),
        out_specs=whole(len(shapes)),
        out_shape=shapes,
        scratch_shapes=[VMEM((rows, depth), jnp.float32)],
        compiler_params=pltpu.CompilerParams(vmem_limit_bytes=LIMIT),
        cost_estimate=cost(0.0, weight),
    )(*parts, weight, *beside)


def unfold(x, spread):
    count = x.shape[0]
    row = lax.broadcasted_iota(jnp.int32, (128, 256), 0)
    col = lax.broadcasted_iota(jnp.int32, (128, 256), 1)
    even = jnp.where(col == 2 * row, 1.0, 0.0).astype(jnp.bfloat16)
    odd = jnp.where(col == 2 * row + 1, 1.0, 0.0).astype(jnp.bfloat16)
    for b in range(x.shape[1] // 128):
        block = x[:, b * 128 : (b + 1) * 128]
        for half, pick in enumerate((even, odd)):
            spread[half * count : (half + 1) * count, b * 256 : (b + 1) * 256] = to_bf16(
                jnp.dot(block, pick, preferred_element_type=jnp.float32)
            )


def query_parts(hidden, gain, w_query, w_kv, n_mem):
    req, depth = hidden.shape
    q_width, kv_width = w_query.shape[1], w_kv.shape[2]
    rows = req // n_mem
    body = q_width + 2 * kv_width
    chunks, ahead = 8, 5
    step = depth // chunks

    def kernel(hid_ref, gain_ref, wq_ref, wkv_ref, *refs):
        outs = refs[:n_mem]
        acc, spread, q_buf, kv_buf, q_sems, kv_sems, hid_buf, gain_buf = refs[n_mem:]
        small = [
            pltpu.make_async_copy(hid_ref, hid_buf, kv_sems.at[1]),
            pltpu.make_async_copy(gain_ref, gain_buf, kv_sems.at[2]),
        ]
        for copy in small:
            copy.start()
        kv_copy = pltpu.make_async_copy(wkv_ref, kv_buf, kv_sems.at[0])
        kv_copy.start()
        copies = [
            pltpu.make_async_copy(
                wq_ref.at[pl.ds(i * step, step)], q_buf.at[pl.ds(i * step, step)], q_sems.at[i]
            )
            for i in range(chunks)
        ]
        for copy in copies[:ahead]:
            copy.start()
        for copy in small:
            copy.wait()
        wide = hid_buf[...].astype(jnp.float32)
        acc[:, body:] = jnp.broadcast_to(jnp.sum(wide * wide, 1, keepdims=True), (req, 128))
        normed = to_bf16(wide * gain_buf[...].astype(jnp.float32).reshape(1, depth))
        unfold(normed, spread)
        for i, copy in enumerate(copies):
            copy.wait()
            if i + ahead < chunks:
                copies[i + ahead].start()
            term = jnp.dot(
                normed[:, i * step : (i + 1) * step],
                q_buf[i * step : (i + 1) * step, :],
                preferred_element_type=jnp.float32,
            )
            acc[:, :q_width] = term if i == 0 else acc[:, :q_width] + term
        kv_copy.wait()
        both = jnp.dot(
            spread[...],
            kv_buf[...].reshape(2 * depth, kv_width),
            preferred_element_type=jnp.float32,
        )
        acc[:, q_width : q_width + kv_width] = both[:req]
        acc[:, q_width + kv_width : body] = both[req:]
        me = lax.axis_index("mem")
        for step_to in range(n_mem):
            at = pl.multiple_of(lax.rem(me + step_to, n_mem) * rows, rows)
            outs[step_to][...] = acc[pl.ds(at, rows), :]

    return pl.pallas_call(
        kernel,
        in_specs=[pl.BlockSpec(memory_space=pltpu.HBM)] * 4,
        out_specs=whole(n_mem),
        out_shape=[jax.ShapeDtypeStruct((rows, body + 128), jnp.float32)] * n_mem,
        scratch_shapes=[
            VMEM((req, body + 128), jnp.float32),
            VMEM((2 * req, 2 * depth), jnp.bfloat16),
            VMEM(w_query.shape, jnp.bfloat16),
            VMEM(w_kv.shape, jnp.bfloat16),
            pltpu.SemaphoreType.DMA((chunks,)),
            pltpu.SemaphoreType.DMA((3,)),
            VMEM(hidden.shape, jnp.bfloat16),
            VMEM(gain.shape, jnp.bfloat16),
        ],
        compiler_params=pltpu.CompilerParams(vmem_limit_bytes=QUERY_LIMIT),
        cost_estimate=pl.CostEstimate(
            flops=2 * req * w_query.size, bytes_accessed=2 * w_query.size, transcendentals=0
        ),
    )(hidden, gain, w_query, w_kv)


def turned_parts(parts, cosine, sine, q_width, kv_width, beside):
    rows = parts[0].shape[0]
    body = q_width + 2 * kv_width
    n = len(parts)

    def kernel(*refs):
        cos_ref, sin_ref, out = refs[n], refs[n + 1], refs[-1]
        total = refs[0][...]
        for ref in refs[1:n]:
            total = total + ref[...]
        scale = lax.rsqrt(total[:, body : body + 1] / D + NORM_EPS)
        cos, sin = cos_ref[...], sin_ref[...]
        for at in range(0, q_width + kv_width, HD):
            head = total[:, at : at + HD] * scale
            out[:, at : at + HD] = to_bf16(head * cos + pltpu.roll(head, HD // 2, 1) * sin)
        out[:, q_width + kv_width :] = to_bf16(total[:, q_width + kv_width : body] * scale)

    return pl.pallas_call(
        kernel,
        in_specs=whole(n + 2) + [pl.BlockSpec(memory_space=pl.ANY)] * len(beside),
        out_specs=pl.BlockSpec(memory_space=VMEM),
        out_shape=jax.ShapeDtypeStruct((rows, body), jnp.bfloat16),
        compiler_params=pltpu.CompilerParams(vmem_limit_bytes=LIMIT),
        cost_estimate=cost(0.0),
    )(*parts, cosine, sine, *beside)


def gate_up_parts(hidden, near, far, gain, held, weight, n_mem, hidden_us):
    req, depth = hidden.shape
    ff = weight.shape[2]
    rows = req // n_mem
    tile = ff // 2 if ff % 256 == 0 else 128

    n_held = len(held)
    first = sum(h.shape[0] for h in held)
    rest = depth - first
    chunk = 128

    def kernel(hid_ref, near_ref, far_ref, gain_ref, *refs):
        held_refs, w_ref, mid_ref = refs[:n_held], refs[n_held], refs[n_held + 1]
        outs, (spread, acc, power, tail, sems) = (
            refs[n_held + 2 : n_held + 2 + n_mem],
            refs[n_held + 2 + n_mem :],
        )
        copies = [
            pltpu.make_async_copy(
                w_ref.at[pl.ds(first + i * chunk, chunk)],
                tail.at[pl.ds(i * chunk, chunk)],
                sems.at[i],
            )
            for i in range(rest // chunk)
        ]
        for copy in copies:
            copy.start()
        total = near_ref[...].astype(jnp.float32) + far_ref[...].astype(jnp.float32)
        middle = to_bf16(hid_ref[...].astype(jnp.float32) + total)
        mid_ref[...] = middle
        wide = middle.astype(jnp.float32)
        power[...] = jnp.broadcast_to(jnp.sum(wide * wide, 1, keepdims=True), power.shape)
        normed = to_bf16(wide * gain_ref[...].astype(jnp.float32).reshape(1, depth))
        unfold(normed, spread)

        def add_rows(block, at, count, fresh):
            @pl.loop(0, ff // tile)
            def _(i):
                cols = pl.ds(pl.multiple_of(i * tile, tile), tile)
                term = jnp.dot(
                    spread[:, 2 * at : 2 * (at + count)],
                    block[:, :, cols].reshape(2 * count, tile),
                    preferred_element_type=jnp.float32,
                )
                acc[:, cols] = term if fresh else acc[:, cols] + term

        at = 0
        for ref in held_refs:
            add_rows(ref, at, ref.shape[0], at == 0)
            at += ref.shape[0]
        for copy in copies:
            copy.wait()
        if rest:
            add_rows(tail, first, rest, first == 0)

        me = lax.axis_index("mem")
        for step in range(n_mem):
            at = pl.multiple_of(lax.rem(me + step, n_mem) * rows, rows)
            out = outs[step]
            gate = acc[pl.ds(at, rows), :]
            up = acc[pl.ds(at + req, rows), :]
            out[:, :ff] = to_bf16(jnp.concatenate([gate, up], 0))
            pw = power[pl.ds(at, rows), :]
            hi = to_bf16(pw).astype(jnp.float32)
            out[:, ff:] = to_bf16(jnp.concatenate([hi, pw - hi], 0))

    return pl.pallas_call(
        kernel,
        in_specs=whole(4 + n_held) + [pl.BlockSpec(memory_space=pl.ANY)],
        out_specs=whole(n_mem + 1),
        out_shape=[jax.ShapeDtypeStruct((req, depth), jnp.bfloat16)]
        + [jax.ShapeDtypeStruct((2 * rows, ff + 128), jnp.bfloat16)] * n_mem,
        scratch_shapes=[
            VMEM((2 * req, 2 * depth), jnp.bfloat16),
            VMEM((2 * req, ff), jnp.float32),
            VMEM((req, 128), jnp.float32),
            VMEM((max(rest, chunk), 2, ff), jnp.bfloat16),
            pltpu.SemaphoreType.DMA((max(rest // chunk, 1),)),
        ],
        compiler_params=pltpu.CompilerParams(vmem_limit_bytes=GATE_LIMIT),
        cost_estimate=cost(hidden_us, weight, 64),
    )(hidden, near, far, gain, *held, weight)


def activate(parts, beside):
    rows = parts[0].shape[0] // 2
    ff = parts[0].shape[1] - 128

    def kernel(*refs):
        out = refs[-1]
        total = refs[0][...].astype(jnp.float32)
        for ref in refs[1 : len(parts)]:
            total = total + ref[...].astype(jnp.float32)
        power = total[:rows, ff : ff + 1] + total[rows:, ff : ff + 1]
        scale = lax.rsqrt(power / D + NORM_EPS)
        gate = total[:rows, :ff] * scale
        up = total[rows:, :ff] * scale
        out[...] = to_bf16(gate / (1.0 + jnp.exp(-gate)) * up)

    return pl.pallas_call(
        kernel,
        in_specs=whole(len(parts)) + [pl.BlockSpec(memory_space=pl.ANY)] * len(beside),
        out_specs=pl.BlockSpec(memory_space=VMEM),
        out_shape=jax.ShapeDtypeStruct((rows, ff), jnp.bfloat16),
        compiler_params=pltpu.CompilerParams(vmem_limit_bytes=LIMIT),
        cost_estimate=cost(0.0),
    )(*parts, *beside)


def around(x, axis, n):
    return [x] + [shifted(x, axis, n, step) for step in range(1, n)]


def added(left, right, hidden_us):
    def kernel(l_ref, r_ref, out):
        out[...] = to_bf16(l_ref[...].astype(jnp.float32) + r_ref[...].astype(jnp.float32))

    return pl.pallas_call(
        kernel,
        in_specs=whole(2),
        out_specs=pl.BlockSpec(memory_space=VMEM),
        out_shape=jax.ShapeDtypeStruct(left.shape, left.dtype),
        compiler_params=pltpu.CompilerParams(vmem_limit_bytes=LIMIT),
        cost_estimate=cost(hidden_us),
    )(left, right)


def pairwise(x, n, hidden_us):
    near, step = x, 1
    while True:
        far = lax.ppermute(near, "comp", [(i, i ^ step) for i in range(n)])
        step *= 2
        if step >= n:
            return near, far
        near = added(near, far, hidden_us)


def rotary(positions, head_dim):
    half_dim = head_dim // 2
    freq_steps = jnp.arange(half_dim, dtype=jnp.float32) * (2.0 / head_dim)
    inv_freq = jnp.exp(-freq_steps * math.log(ROPE_BASE))
    angles = positions.astype(jnp.float32)[:, None, None] * inv_freq
    return jnp.cos(angles), jnp.sin(angles)


def rotate(values, cosine, sine):
    half_dim = values.shape[-1] // 2
    first_half = values[..., :half_dim]
    second_half = values[..., half_dim:]
    return jnp.concatenate(
        [first_half * cosine - second_half * sine, second_half * cosine + first_half * sine], -1
    )


def slot_stats(queries_slot, key_rows, value_rows, slot_fill, scale_val):
    scores = (
        jnp.einsum("skgd,sbkd->skgb", queries_slot, key_rows, preferred_element_type=jnp.float32)
        * scale_val
    )
    is_valid = (jnp.arange(key_rows.shape[1], dtype=jnp.int32)[None, :] < slot_fill[:, None])[
        :, None, None, :
    ]
    scores = jnp.where(is_valid, scores, NEG_FILL)
    peak_val = jnp.max(scores, -1)
    weights = jnp.where(is_valid, jnp.exp(scores - peak_val[..., None]), 0.0)
    total_w = jnp.sum(weights, -1)
    weighted = jnp.einsum(
        "skgb,sbkd->skgd",
        weights.astype(jnp.bfloat16),
        value_rows,
        preferred_element_type=jnp.float32,
    )
    return (peak_val, total_w, weighted)


def make_shards(n_mem, n_comp):
    def shards(
        hidden_in,
        lengths,
        block_table,
        cache_keys,
        cache_values,
        attn_gain,
        w_query,
        w_kv,
        w_out,
        ffn_gain,
        w_gate_up,
        w_down,
    ):
        highest = lax.Precision.HIGHEST
        req_count = hidden_in.shape[0]
        slot_count, blk_len, kv_width = cache_keys.shape
        head_dim = HD
        kv_local = kv_width // head_dim
        q_width = w_query.shape[1]
        group_size = q_width // kv_width
        scale_val = 1.0 / math.sqrt(head_dim)
        mem_pos = lax.axis_index("mem")
        rows = req_count // n_mem
        if rows % 8:
            resid = hidden_in.astype(jnp.float32)
            normed = to_bf16(resid * attn_gain.astype(jnp.float32))
            query_part = jnp.dot(normed, w_query, preferred_element_type=jnp.float32)
            kv_part = jnp.dot(
                normed, w_kv.reshape(w_kv.shape[0], -1), preferred_element_type=jnp.float32
            )
            power = jnp.sum(resid * resid, 1)
            wide = jnp.concatenate(
                [query_part, kv_part, jnp.broadcast_to(power[:, None], (req_count, 128))], 1
            ).reshape(n_mem, rows, -1)
            total = lax.dynamic_index_in_dim(wide, mem_pos, 0, False)
            for part in scatter_parts(wide, "mem", n_mem):
                total = total + part
            body = q_width + 2 * kv_width
            attn_scale = lax.rsqrt(total[:, body] / D + NORM_EPS)
            cosine, sine = rotary(lengths, head_dim)
            cos_own = lax.dynamic_slice_in_dim(cosine, mem_pos * rows, rows, 0)
            sin_own = lax.dynamic_slice_in_dim(sine, mem_pos * rows, rows, 0)
            scaled = total[:, :body] * attn_scale[:, None]
            turned = rotate(
                scaled[:, : q_width + kv_width].reshape(rows, -1, head_dim), cos_own, sin_own
            ).reshape(rows, -1)
            own_qkv = to_bf16(jnp.concatenate([turned, scaled[:, q_width + kv_width :]], 1))
        else:
            here = lax.dynamic_slice_in_dim(lengths, mem_pos * rows, rows, 0)
            cosine, sine = rotary(here, head_dim)
            cosine = jnp.concatenate([cosine, cosine], -1)[:, 0]
            sine = jnp.concatenate([-sine, sine], -1)[:, 0]
            terms = list(query_parts(hidden_in, attn_gain, w_query, w_kv, n_mem))
            out_held = fetch(w_out, 0, w_out.shape[0], terms[0], OUT_LIMIT)
            terms = terms[:1] + [shifted(t, "mem", n_mem, s) for s, t in enumerate(terms) if s]
            own_qkv = turned_parts(terms, cosine, sine, q_width, kv_width, (out_held,))
        qkv = gather_parts(own_qkv, "mem", n_mem)
        queries = qkv[:, :q_width].reshape(req_count, kv_local, group_size, head_dim)
        q_own = own_qkv[:, :q_width].reshape(rows, kv_local, group_size, head_dim)
        new_keys = own_qkv[:, q_width : q_width + kv_width].reshape(rows, kv_local, head_dim)
        new_values = own_qkv[:, q_width + kv_width :].reshape(rows, kv_local, head_dim)
        own_score = (
            jnp.einsum("rkgd,rkd->rkg", q_own, new_keys, preferred_element_type=jnp.float32)
            * scale_val
        )

        blk_count = block_table.shape[1]
        block_first = jnp.arange(blk_count, dtype=jnp.int32) * blk_len
        is_live = block_first[None, :] < lengths[:, None]
        local_slot = block_table - mem_pos * slot_count
        slot_ids = jnp.arange(slot_count, dtype=jnp.int32)
        owners = is_live[:, :, None] & (local_slot[:, :, None] == slot_ids[None, None, :])
        slot_member = jnp.any(owners, 1).T
        block_fill = jnp.clip(lengths[:, None] - block_first[None, :], 0, blk_len)
        slot_fill = jnp.sum(jnp.where(owners, block_fill[:, :, None], 0), (0, 1))
        queries_slot = jnp.dot(
            slot_member.astype(jnp.bfloat16),
            queries.reshape(req_count, -1),
            preferred_element_type=jnp.float32,
        )
        queries_slot = queries_slot.astype(jnp.bfloat16).reshape(
            slot_count, kv_local, group_size, head_dim
        )
        key_rows = cache_keys.reshape(slot_count, blk_len, kv_local, head_dim)
        value_rows = cache_values.reshape(slot_count, blk_len, kv_local, head_dim)
        peak_val, total_w, weighted = slot_stats(
            queries_slot, key_rows, value_rows, slot_fill, scale_val
        )
        member_mask = slot_member[:, :, None, None]
        req_peak = jnp.max(jnp.where(member_mask, peak_val[:, None], NEG_FILL), 0)
        peak_hi = lax.reduce_precision(req_peak, 8, 7)
        peak_lo = lax.reduce_precision(req_peak - peak_hi, 8, 7)
        req_peak = peak_hi + peak_lo
        slot_ref = jnp.min(jnp.where(member_mask, req_peak[None], -NEG_FILL), 1)
        factor = jnp.exp(peak_val - slot_ref)
        member_wide = slot_member.astype(jnp.float32)
        req_total = jnp.einsum("sr,skg->rkg", member_wide, total_w * factor, precision=highest)
        req_weighted = jnp.einsum(
            "sr,skgd->rkgd", member_wide, weighted * factor[..., None], precision=highest
        )
        tot_hi = lax.reduce_precision(req_total, 8, 7)
        tot_lo = req_total - tot_hi
        stats = jnp.concatenate(
            [s.reshape(req_count, -1) for s in (peak_hi, peak_lo, tot_hi, tot_lo)], 1
        )
        n_stat = kv_local * group_size
        pad = (-stats.shape[1]) % 128
        stats = jnp.pad(stats, ((0, 0), (0, pad)))
        packed = to_bf16(jnp.concatenate([req_weighted.reshape(req_count, -1), stats], 1))
        packed = packed.reshape(n_mem, rows, -1)
        pieces = [lax.dynamic_index_in_dim(packed, mem_pos, 0, False)]
        pieces += scatter_parts(packed, "mem", n_mem)
        peaks, totals, tops = [], [], []
        for piece in pieces:
            st = piece[:, q_width : q_width + 4 * n_stat].astype(jnp.float32)
            st = st.reshape(rows, 4, kv_local, group_size)
            peaks.append(st[:, 0] + st[:, 1])
            totals.append(st[:, 2] + st[:, 3])
            tops.append(
                piece[:, :q_width]
                .astype(jnp.float32)
                .reshape(rows, kv_local, group_size, head_dim)
            )
        peak = own_score
        for p in peaks:
            peak = jnp.maximum(peak, p)
        own_weight = jnp.exp(own_score - peak)
        denom = own_weight
        numer = own_weight[..., None] * new_values.astype(jnp.float32)[:, :, None, :]
        for p, t, w in zip(peaks, totals, tops):
            f = jnp.exp(p - peak)
            denom = denom + t * f
            numer = numer + w * f[..., None]
        attended_own = to_bf16(numer / denom[..., None]).reshape(rows, -1)
        if rows % 8:
            attended = gather_parts(attended_own, "mem", n_mem)

            comp_pos = lax.axis_index("comp")
            rows_c = req_count // n_comp
            attn_proj = jnp.dot(attended, w_out, preferred_element_type=jnp.float32)
            resid_own = lax.dynamic_slice_in_dim(hidden_in, comp_pos * rows_c, rows_c, 0)
            middle_own = to_bf16(resid_own.astype(jnp.float32) + summed(attn_proj, "comp", n_comp))
            middle = gather_parts(middle_own, "comp", n_comp)
            middle_wide = middle.astype(jnp.float32)
            normed_ffn = to_bf16(middle_wide * ffn_gain.astype(jnp.float32))
            gate_up = jnp.einsum(
                "rd,dtf->rtf", normed_ffn, w_gate_up, preferred_element_type=jnp.float32
            ).reshape(req_count, -1)
            m_hi, m_lo = split_hi_lo(jnp.sum(middle_wide * middle_wide, 1))
            wide = jnp.concatenate(
                [
                    to_bf16(gate_up),
                    jnp.broadcast_to(m_hi[:, None], (req_count, 128)),
                    jnp.broadcast_to(m_lo[:, None], (req_count, 128)),
                ],
                1,
            ).reshape(n_mem, rows, -1)
            total = lax.dynamic_index_in_dim(wide, mem_pos, 0, False).astype(jnp.float32)
            for part in scatter_parts(wide, "mem", n_mem):
                total = total + part.astype(jnp.float32)
            ff = w_gate_up.shape[2]
            ffn_scale = lax.rsqrt((total[:, 2 * ff] + total[:, 2 * ff + 128]) / D + NORM_EPS)
            gate = total[:, :ff] * ffn_scale[:, None]
            up = total[:, ff : 2 * ff] * ffn_scale[:, None]
            activated = gather_parts(to_bf16(jax.nn.silu(gate) * up), "mem", n_mem)
            down_part = jnp.dot(activated, w_down, preferred_element_type=jnp.float32)
            updated_own = to_bf16(middle_own.astype(jnp.float32) + summed(down_part, "comp", n_comp))
            updated = gather_parts(updated_own, "comp", n_comp)
            return (attended, updated)

        depth = w_gate_up.shape[0]
        cut_a, cut_b = depth * CUT[0] // 16, depth * CUT[1] // 16
        gate_a = fetch(w_gate_up, 0, cut_a, attended_own)
        proj, attended = gathered_dot(
            around(attended_own, "mem", n_mem), out_held, n_mem, True, (gate_a,)
        )
        near, far = pairwise(proj, n_comp, 0.0)
        gate_b = fetch(w_gate_up, cut_a, cut_b, near)
        middle, *terms = gate_up_parts(
            hidden_in, near, far, ffn_gain, (gate_a, gate_b), w_gate_up, n_mem, 0.0
        )
        down_held = fetch(w_down, 0, w_down.shape[0], terms[0])
        terms = terms[:1] + [shifted(t, "mem", n_mem, s) for s, t in enumerate(terms) if s]
        activated = activate(terms, (down_held,))
        (down,) = gathered_dot(
            around(activated, "mem", n_mem), down_held, n_mem, False
        )
        near, far = pairwise(down, n_comp, 0.0)
        updated = to_bf16(
            middle.astype(jnp.float32) + (near.astype(jnp.float32) + far.astype(jnp.float32))
        )
        return (attended, updated)

    return shards


def solution(mesh):
    in_specs = (
        P("groups", "mem"),
        P("groups"),
        P("groups", None),
        P(("groups", "mem"), None, "comp"),
        P(("groups", "mem"), None, "comp"),
        P("mem"),
        P("mem", "comp"),
        P("mem", None, "comp"),
        P("comp", "mem"),
        P("mem"),
        P("mem", None, "comp"),
        P("comp", "mem"),
    )
    out_specs = (P("groups", "comp"), P("groups", "mem"))
    return jax.shard_map(
        make_shards(mesh.shape["mem"], mesh.shape["comp"]),
        mesh=mesh,
        in_specs=in_specs,
        out_specs=out_specs,
        check_vma=False,
    )
```
